512 devices in a mesh: ta: 16 (over x_lo, z), ha: 32 (over y, x_hi, core).
Axes of the slice: x: 4 (x_hi: 2, x_lo: 2; x = x_hi * 2 + x_lo), y: 8, z: 8, core: 2. Of those that a mesh axis runs over, the one named last changes fastest.
Arguments:
- queries: bfloat16 [16, 512, 8, 2048], P('ta', 'ha'), may hold values from -6 to 6
- keys: bfloat16 [16, 512, 8, 2048], P('ta', 'ha'), may hold values from -6 to 6
- values: bfloat16 [16, 512, 8, 2048], P('ta', 'ha'), may hold values from -6 to 6
- out_grad: bfloat16 [16, 512, 8, 2048], P('ta', 'ha'), may hold values from -96 to 96
- log_sum_exp: float32 [16, 16, 4096], P(None, 'ta', 'ha'), may hold values from 7.3 to 8.5
- row_delta: float32 [16, 16, 4096], P(None, 'ta', 'ha'), may hold values from -600 to 600
- time_start: int32 [16, 4], replicated, may hold values from 0 to 1, as said below
- height_start: int32 [16, 64], replicated, may hold values from 0 to 61, as said below
- head_order: int32 [16], replicated, may hold values from 0 to 15, each once
Outputs:
- query_grad: bfloat16 [16, 512, 8, 2048], P('ta', 'ha')
- key_grad: bfloat16 [16, 512, 8, 2048], P('ta', 'ha')
- value_grad: bfloat16 [16, 512, 8, 2048], P('ta', 'ha')
The draws below stay inside these ranges and needn't reach their ends.
Inputs may be any that keep to these rules, and one draw needn't show every extreme that they name: time_start[m, a] lies between a - 2 and a, so the window holds tile a. height_start[m, c] lies between c - 2 and c, so the window holds tile c. `head_order`: each model head appears in exactly one slot.
All inputs are finite; a program needn't handle non-finite values.
Results may differ from the reference program's by a relative error of at most 0.0054.
Values may be sent and summed in bfloat16 or wider, within the bound.
A program may use at most 64 MiB of HBM per device.

```python
import jax
import jax.numpy as jnp
from jax import lax

HEADS = 16
HD = 128
TILE_T = 4
TILE_H = 8
TILE_W = 8
FRAMES = 16
HEIGHT = 512


def window_starts(key, head_count, tile_count):
    offset = jax.random.randint(key, (head_count, tile_count), -1, 2, dtype=jnp.int32)
    tile_index = jnp.arange(tile_count, dtype=jnp.int32)[None, :]
    return jnp.clip(tile_index - 1 + offset, 0, tile_count - 3).astype(jnp.int32)


def draw_time_start(key, part):
    key = jax.random.fold_in(key, 11)
    return window_starts(key, HEADS, FRAMES // TILE_T)


def draw_height_start(key, part):
    key = jax.random.fold_in(key, 23)
    return window_starts(key, HEADS, HEIGHT // TILE_H)


def block_levels(own_key, shape, pieces, low, high):
    def one(axis_at, blocks):
        heights = jax.random.uniform(jax.random.fold_in(jax.random.fold_in(own_key, 6), axis_at), (blocks,), jnp.float32, low / len(pieces), high / len(pieces))
        return jnp.repeat(jnp.exp(heights), shape[axis_at] // blocks).reshape((-1,) + (1,) * (len(shape) - axis_at - 1))

    factor_of = one(*pieces[0])
    for cut in pieces[1:]:
        factor_of = factor_of * one(*cut)
    return factor_of


def noise(own_key, dims, width, limit, shards=(), held_as=jnp.bfloat16):
    factor_of = block_levels(own_key, dims, shards, -0.22, 0.18) if shards else 1.0
    drawn = jax.random.normal(own_key, dims, jnp.float32) * width * factor_of
    return jnp.minimum(jnp.maximum(drawn, -limit), limit).astype(held_as)


def setup_inputs(seed: int = 0) -> dict:
    seeds = jax.random.split(jax.random.key(seed), 10)
    queries = noise(seeds[0], (FRAMES, HEIGHT, TILE_W, HEADS * HD), 1.0, 6.0, ((0, 16), (1, 32)))
    keys = noise(seeds[1], (FRAMES, HEIGHT, TILE_W, HEADS * HD), 1.0, 6.0, ((0, 16), (1, 32)))
    values = noise(seeds[2], (FRAMES, HEIGHT, TILE_W, HEADS * HD), 1.0, 6.0, ((0, 16), (1, 32)))
    out_grad = noise(seeds[3], (FRAMES, HEIGHT, TILE_W, HEADS * HD), 16.0, 96.0, ((0, 16), (1, 32)))
    log_sum_exp = jnp.clip(7.3 + 1.1999998 * jax.random.uniform(seeds[4], (HEADS, FRAMES, HEIGHT * TILE_W), jnp.float32) ** block_levels(seeds[4], (HEADS, FRAMES, HEIGHT * TILE_W), ((1, 16), (2, 32)), -0.2, 0.2), 7.3, 8.5)
    row_delta = noise(seeds[5], (HEADS, FRAMES, HEIGHT * TILE_W), 100.0, 600.0, ((1, 16), (2, 32)), jnp.float32)
    time_start = draw_time_start(jax.random.fold_in(seeds[9], 71), 0)
    height_start = draw_height_start(jax.random.fold_in(seeds[9], 71), 0)
    head_order = jax.random.permutation(seeds[8], HEADS).astype(jnp.int32)
    return {"queries": queries, "keys": keys, "values": values, "out_grad": out_grad, "log_sum_exp": log_sum_exp, "row_delta": row_delta, "time_start": time_start, "height_start": height_start, "head_order": head_order}


def tile_grads(query_tile, grad_tile, lse_tile, delta_tile, key_window, value_window):
    factor = HD ** -0.5
    scores = jnp.dot(query_tile, key_window.T, preferred_element_type=jnp.float32) * factor
    probs_high = jnp.exp(scores - lse_tile[:, None])
    probs_low = probs_high.astype(jnp.bfloat16)
    dprob_high = jnp.dot(grad_tile, value_window.T, preferred_element_type=jnp.float32)
    dscore = probs_high * (dprob_high - delta_tile[:, None])
    dscore_low = dscore.astype(jnp.bfloat16)
    query_part = factor * jnp.dot(dscore_low, key_window, preferred_element_type=jnp.float32)
    key_part = factor * jnp.dot(dscore_low.T, query_tile, preferred_element_type=jnp.float32)
    value_part = jnp.dot(probs_low.T, grad_tile, preferred_element_type=jnp.float32)
    return query_part, key_part, value_part


def to_tiles(tensor):
    frames, height, tile_width, features = tensor.shape
    time_tiles = frames // TILE_T
    height_tiles = height // TILE_H
    head_count = features // HD
    shaped = tensor.reshape(time_tiles, TILE_T, height_tiles, TILE_H, tile_width, head_count, HD)
    shaped = shaped.transpose(5, 0, 2, 1, 3, 4, 6)
    return shaped.reshape(head_count, time_tiles, height_tiles, TILE_T * TILE_H * tile_width, HD)


def from_tiles(tiled, tile_width):
    head_count, time_tiles, height_tiles, tile_size, head_depth = tiled.shape
    shaped = tiled.reshape(head_count, time_tiles, height_tiles, TILE_T, TILE_H, tile_width, head_depth)
    shaped = shaped.transpose(1, 3, 2, 4, 5, 0, 6)
    return shaped.reshape(time_tiles * TILE_T, height_tiles * TILE_H, tile_width, head_count * head_depth)


def stat_tiles(stat_rows, tile_width):
    head_count, frames, cells = stat_rows.shape
    time_tiles = frames // TILE_T
    height_tiles = cells // (TILE_H * tile_width)
    shaped = stat_rows.reshape(head_count, time_tiles, TILE_T, height_tiles, TILE_H * tile_width)
    shaped = shaped.transpose(0, 1, 3, 2, 4)
    return shaped.reshape(head_count, time_tiles, height_tiles, TILE_T * TILE_H * tile_width)


def reference(queries, keys, values, out_grad, log_sum_exp, row_delta, time_start, height_start, head_order):
    tile_width = queries.shape[2]
    query_tiles = to_tiles(queries)
    key_tiles = to_tiles(keys)
    value_tiles = to_tiles(values)
    grad_tiles = to_tiles(out_grad)
    lse_tiles = stat_tiles(log_sum_exp, tile_width)
    delta_tiles = stat_tiles(row_delta, tile_width)
    time_tiles = query_tiles.shape[1]
    height_tiles = query_tiles.shape[2]
    tile_size = query_tiles.shape[3]

    def one_head(head_query, head_keys, head_values, head_grad, head_lse, head_delta, time_rows, height_rows):
        zero_grads = jnp.zeros((time_tiles, height_tiles, tile_size, HD), jnp.float32)

        def visit_tile(running, position):
            key_sums, value_sums = running
            time_tile = position // height_tiles
            height_tile = position % height_tiles
            anchor = (time_rows[time_tile], height_rows[height_tile], jnp.int32(0), jnp.int32(0))
            key_window = lax.dynamic_slice(head_keys, anchor, (3, 3, tile_size, HD)).reshape(9 * tile_size, HD)
            value_window = lax.dynamic_slice(head_values, anchor, (3, 3, tile_size, HD)).reshape(9 * tile_size, HD)
            query_part, key_part, value_part = tile_grads(
                head_query[time_tile, height_tile], head_grad[time_tile, height_tile],
                head_lse[time_tile, height_tile], head_delta[time_tile, height_tile],
                key_window, value_window)
            key_old = lax.dynamic_slice(key_sums, anchor, (3, 3, tile_size, HD))
            key_sums = lax.dynamic_update_slice(key_sums, key_old + key_part.reshape(3, 3, tile_size, HD), anchor)
            value_old = lax.dynamic_slice(value_sums, anchor, (3, 3, tile_size, HD))
            value_sums = lax.dynamic_update_slice(value_sums, value_old + value_part.reshape(3, 3, tile_size, HD), anchor)
            return (key_sums, value_sums), query_part.astype(jnp.bfloat16)

        positions = jnp.arange(time_tiles * height_tiles, dtype=jnp.int32)
        (key_sums, value_sums), query_parts = lax.scan(visit_tile, (zero_grads, zero_grads), positions)
        query_out = query_parts.reshape(time_tiles, height_tiles, tile_size, HD)
        return query_out, key_sums.astype(jnp.bfloat16), value_sums.astype(jnp.bfloat16)

    time_rows = time_start[head_order]
    height_rows = height_start[head_order]
    query_all, key_all, value_all = jax.vmap(one_head)(
        query_tiles, key_tiles, value_tiles, grad_tiles, lse_tiles, delta_tiles, time_rows, height_rows)
    return from_tiles(query_all, tile_width), from_tiles(key_all, tile_width), from_tiles(value_all, tile_width)
```

```python
import functools

import jax
import jax.numpy as jnp
from jax import lax
from jax.experimental import pallas as pl
from jax.experimental.pallas import tpu as pltpu
from jax.sharding import PartitionSpec as P

HD = 128
SCALE = HD ** -0.5
LOG2E = 1.4426950408889634
NT = 16
NH = 32
TOK = 128
HALF = 64
SPAN = 3 * HALF
MESH = pl.DeviceIdType.MESH


def dot(a, b, dims):
    return lax.dot_general(a, b, (dims, ((), ())), preferred_element_type=jnp.float32)


def grads_kernel(
    order, time_start, height_start, lse, delta, queries, keys, values, out_grad,
    query_out, key_out, value_out,
    key_buf, value_buf, query_buf, grad_buf, lse_buf, delta_buf,
    key_window, value_window, key_parts, value_parts, key_sum, value_sum,
    query_low, key_low, value_low,
    key_send, value_send, key_recv, value_recv,
    stat_ss, stat_rs, kv_ss, kv_rs, qg_ss, qg_rs, own_sem,
    halo_ss, halo_rs, back_ss, back_rs, qo_ss, qo_rs, kvo_ss, kvo_rs,
):
    ta = lax.axis_index("ta")
    ha = lax.axis_index("ha")
    core = lax.rem(ha, 2)
    x_hi = lax.rem(ha // 2, 2)
    head = lax.rem(ta + 8 * x_hi, NT)

    def peer(d):
        return lax.rem(ta + d, NT)

    def head_of(p):
        return lax.rem(p + 8 * x_hi, NT)

    def columns(h):
        return pl.ds(pl.multiple_of(h * HD, HD), HD)

    left = (lax.rem(ta + 8 * (1 - core), NT), lax.rem(ha + NH - 1, NH))
    right = (lax.rem(ta + 8 * core, NT), lax.rem(ha + 1, NH))
    sides = (left, right)

    barrier = pltpu.get_barrier_semaphore()

    @pl.loop(1, NT)
    def _(d):
        pl.semaphore_signal(barrier, inc=1, device_id=(peer(d), ha), device_id_type=MESH)

    for side in sides:
        pl.semaphore_signal(barrier, inc=1, device_id=side, device_id_type=MESH)
    pl.semaphore_wait(barrier, NT + 1)

    def remote(src, dst, send_sem, recv_sem, device):
        return pltpu.make_async_remote_copy(
            src_ref=src, dst_ref=dst, send_sem=send_sem, recv_sem=recv_sem,
            device_id=device, device_id_type=MESH,
        )

    def stat_copy(n, d):
        p = peer(d)
        src, dst = ((lse, lse_buf), (delta, delta_buf))[n]
        return remote(src.at[head_of(p)], dst.at[ta], stat_ss.at[n, d], stat_rs.at[n, d], (p, ha))

    def kv_copy(n, d):
        p = peer(d)
        src, dst = ((keys, key_buf), (values, value_buf))[n]
        return remote(
            src.at[:, columns(head_of(p))], dst.at[ta, pl.ds(TOK, TOK), :],
            kv_ss.at[n, d], kv_rs.at[n, d], (p, ha),
        )

    def qg_copy(n, c, d):
        p = peer(d)
        src, dst = ((queries, query_buf), (out_grad, grad_buf))[n]
        return remote(
            src.at[pl.ds(c * HALF, HALF), columns(head_of(p))], dst.at[c, ta],
            qg_ss.at[n, c, d], qg_rs.at[n, c, d], (p, ha),
        )

    own = [
        pltpu.make_async_copy(keys.at[:, columns(head)], key_buf.at[ta, pl.ds(TOK, TOK), :], own_sem.at[0]),
        pltpu.make_async_copy(values.at[:, columns(head)], value_buf.at[ta, pl.ds(TOK, TOK), :], own_sem.at[1]),
        pltpu.make_async_copy(lse.at[head], lse_buf.at[ta], own_sem.at[2]),
        pltpu.make_async_copy(delta.at[head], delta_buf.at[ta], own_sem.at[3]),
    ]
    for c in range(2):
        for n, (src, dst) in enumerate(((queries, query_buf), (out_grad, grad_buf))):
            own.append(
                pltpu.make_async_copy(
                    src.at[pl.ds(c * HALF, HALF), columns(head)], dst.at[c, ta], own_sem.at[4 + 2 * c + n]
                )
            )

    for n in range(2):
        @pl.loop(1, NT)
        def _(d, n=n):
            kv_copy(n, d).start()
    for n in range(2):
        @pl.loop(1, NT)
        def _(d, n=n):
            stat_copy(n, d).start()
    for c in range(2):
        for n in range(2):
            @pl.loop(1, NT)
            def _(d, n=n, c=c):
                qg_copy(n, c, d).start()
    for copy in own:
        copy.start()

    for copy in own:
        copy.wait()

    halos = []
    for n, buf in enumerate((key_buf, value_buf)):
        @pl.loop(1, NT)
        def _(d, n=n):
            kv_copy(n, d).wait_recv()

        for s in range(2):
            copy = remote(
                buf.at[:, pl.ds(TOK, TOK), :],
                buf.at[:, pl.ds(2 * TOK * (1 - s), TOK), :],
                halo_ss.at[n, s], halo_rs.at[n, s], sides[s],
            )
            copy.start()
            halos.append(copy)

    for n in range(2):
        @pl.loop(1, NT)
        def _(d, n=n):
            stat_copy(n, d).wait_recv()
    for copy in halos:
        copy.wait_recv()

    model_head = order[head]

    def pick(table, column):
        entry = table[0, column]
        for m in range(1, NT):
            entry = jnp.where(model_head == m, table[m, column], entry)
        return entry

    early = [None] + [pick(time_start, a) == 0 for a in (1, 2)]
    low_lane = lax.broadcasted_iota(jnp.int32, (1, HD), 1) < HALF

    def stat_row(buf, a, c):
        rows = [buf[4 * a + i] for i in range(4)]
        flipped = [pltpu.roll(row, HALF, 1) for row in rows]
        if c == 0:
            pairs = [jnp.where(low_lane, rows[2 * i], flipped[2 * i + 1]) for i in range(2)]
        else:
            pairs = [jnp.where(low_lane, flipped[2 * i], rows[2 * i + 1]) for i in range(2)]
        return jnp.concatenate(pairs, axis=1)

    def query_copy(c, frame):
        return remote(
            query_low.at[c, frame], query_out.at[pl.ds(c * HALF, HALF), columns(head)],
            qo_ss.at[c, frame], qo_rs.at[c, ta], (frame, ha),
        )

    def query_own(c):
        return pltpu.make_async_copy(
            query_low.at[c, ta], query_out.at[pl.ds(c * HALF, HALF), columns(head)], qo_ss.at[c, ta]
        )

    for c in range(2):
        for n in range(2):
            @pl.loop(1, NT)
            def _(d, n=n, c=c):
                qg_copy(n, c, d).wait_recv()

        step = pick(height_start, 2 * ha + c) - (2 * ha + c) + 2
        at = [step == d for d in range(3)]

        @pl.loop(0, NT)
        def _(frame, c=c, at=at):
            for buf, window in ((key_buf, key_window), (value_buf, value_window)):
                spans = [buf[frame, pl.ds(HALF * (c + d), SPAN), :] for d in range(3)]
                window[frame] = jnp.where(at[0], spans[0], jnp.where(at[1], spans[1], spans[2]))

        @pl.loop(0, 4)
        def _(a, c=c):
            soon = pick(time_start, a) == 0

            def tile(window, j):
                now = window[pl.ds(4 * j, 4)]
                later = window[pl.ds(4 * j + 4, 4)]
                return jnp.where(soon, now, later).reshape(4 * SPAN, HD)

            query = query_buf[c, pl.ds(4 * a, 4)].reshape(4 * HALF, HD)
            grad = grad_buf[c, pl.ds(4 * a, 4)].reshape(4 * HALF, HD)
            lse_row = stat_row(lse_buf, a, c) * LOG2E
            delta_row = stat_row(delta_buf, a, c)
            turned = jnp.zeros((HD, 4 * HALF), jnp.float32)
            for j in range(3):
                key = tile(key_window, j)
                value = tile(value_window, j)
                scores = dot(key, query, ((1,), (1,)))
                probs = jnp.exp2(scores * (SCALE * LOG2E) - lse_row)
                dprob = dot(value, grad, ((1,), (1,)))
                dscore = (probs * (dprob - delta_row)).astype(jnp.bfloat16)
                value_parts[3 * a + j] = dot(
                    probs.astype(jnp.bfloat16), grad, ((1,), (0,))
                ).reshape(4, SPAN, HD)
                key_parts[3 * a + j] = dot(dscore, query, ((1,), (0,))).reshape(4, SPAN, HD)
                turned = turned + dot(key, dscore, ((0,), (0,)))
            query_low[c, pl.ds(4 * a, 4)] = (
                (turned.T * SCALE).astype(jnp.bfloat16).reshape(4, HALF, HD)
            )
            for i in range(4):
                frame = 4 * a + i

                @pl.when(frame != ta)
                def _(frame=frame):
                    query_copy(c, frame).start()

                @pl.when(frame == ta)
                def _():
                    query_own(c).start()

        back = []
        for n, (parts, total, send) in enumerate(
            ((key_parts, key_sum, key_send), (value_parts, value_sum, value_send))
        ):
            for t in range(4):
                @pl.loop(0, 4)
                def _(i, parts=parts, total=total, send=send, t=t, c=c, at=at):
                    frame = 4 * t + i
                    blank = jnp.zeros((SPAN, HD), jnp.float32)
                    found = blank
                    for a in range(4):
                        now = parts[3 * a + t, i] if t < 3 and a < 3 else blank
                        later = parts[3 * a + t - 1, i] if t > 0 and a > 0 else blank
                        if a == 0:
                            found = now
                        elif a == 3:
                            found = found + later
                        else:
                            found = found + jnp.where(early[a], now, later)
                    one, two, three = (found[HALF * e : HALF * (e + 1)] for e in range(3))
                    none = blank[:HALF]
                    placed = [
                        jnp.where(at[0], one, none),
                        jnp.where(at[0], two, jnp.where(at[1], one, none)),
                        jnp.where(at[0], three, jnp.where(at[1], two, one)),
                        jnp.where(at[1], three, jnp.where(at[2], two, none)),
                        jnp.where(at[2], three, none),
                    ]
                    if c == 0:
                        for e in range(5):
                            total[frame, HALF * e : HALF * (e + 1), :] = placed[e]
                    else:
                        low = jnp.bfloat16
                        both = [total[frame, HALF * e : HALF * (e + 1), :] + placed[e - 1] for e in range(1, 5)]
                        send[0, frame, 0:HALF, :] = total[frame, 0:HALF, :].astype(low)
                        send[0, frame, HALF:TOK, :] = both[0].astype(low)
                        total[frame, TOK : TOK + HALF, :] = both[1]
                        total[frame, TOK + HALF : 2 * TOK, :] = both[2]
                        send[1, frame, 0:HALF, :] = both[3].astype(low)
                        send[1, frame, HALF:TOK, :] = placed[4].astype(low)

            if c == 1:
                recv = (key_recv, value_recv)[n]
                for s in range(2):
                    copy = remote(
                        send.at[s], recv.at[1 - s], back_ss.at[n, s], back_rs.at[n, 1 - s], sides[s]
                    )
                    copy.start()
                    back.append(copy)

    def grad_copy(n, d):
        p = peer(d)
        low, out = ((key_low, key_out), (value_low, value_out))[n]
        return remote(
            low.at[p], out.at[:, columns(head)], kvo_ss.at[n, d], kvo_rs.at[n, d], (p, ha)
        )

    own_out = []
    for n, (total, recv, low, out) in enumerate(
        ((key_sum, key_recv, key_low, key_out), (value_sum, value_recv, value_low, value_out))
    ):
        for s in range(2):
            back[2 * n + s].wait_recv()
        factor = SCALE if n == 0 else 1.0

        @pl.loop(0, NT)
        def _(frame, total=total, recv=recv, low=low, factor=factor):
            whole = (
                total[frame, 128:256, :]
                + recv[0, frame].astype(jnp.float32)
                + recv[1, frame].astype(jnp.float32)
            )
            low[frame] = (whole * factor).astype(jnp.bfloat16)

        @pl.loop(1, NT)
        def _(d, n=n):
            grad_copy(n, d).start()

        copy = pltpu.make_async_copy(low.at[ta], out.at[:, columns(head)], own_sem.at[n])
        copy.start()
        own_out.append(copy)

    for n in range(2):
        @pl.loop(1, NT)
        def _(d, n=n):
            stat_copy(n, d).wait_send()
            kv_copy(n, d).wait_send()
            for c in range(2):
                qg_copy(n, c, d).wait_send()
    for copy in halos + back:
        copy.wait_send()
    for c in range(2):
        query_own(c).wait()

        @pl.loop(1, NT)
        def _(d, c=c):
            frame = peer(d)
            done = remote(
                query_low.at[c, frame], query_out.at[pl.ds(c * HALF, HALF), columns(head_of(frame))],
                qo_ss.at[c, frame], qo_rs.at[c, frame], (frame, ha),
            )
            done.wait_send()
            done.wait_recv()

    for n in range(2):
        @pl.loop(1, NT)
        def _(d, n=n):
            grad_copy(n, d).wait()

    for copy in own_out:
        copy.wait()


def per_device(
    queries, keys, values, out_grad, log_sum_exp, row_delta, time_start, height_start, head_order
):
    width = NT * HD
    flat = [x.reshape(TOK, width) for x in (queries, keys, values, out_grad)]
    smem = pl.BlockSpec(memory_space=pltpu.SMEM)
    hbm = pl.BlockSpec(memory_space=pl.ANY)
    bf16, f32 = jnp.bfloat16, jnp.float32
    dma = pltpu.SemaphoreType.DMA
    outs = pl.pallas_call(
        grads_kernel,
        name="tile_attention_grads",
        out_shape=[jax.ShapeDtypeStruct((TOK, width), bf16)] * 3,
        in_specs=[smem] * 3 + [hbm] * 6,
        out_specs=[hbm] * 3,
        scratch_shapes=[
            pltpu.VMEM((NT, 3 * TOK, HD), bf16),
            pltpu.VMEM((NT, 3 * TOK, HD), bf16),
            pltpu.VMEM((2, NT, HALF, HD), bf16),
            pltpu.VMEM((2, NT, HALF, HD), bf16),
            pltpu.VMEM((NT, 1, TOK), f32),
            pltpu.VMEM((NT, 1, TOK), f32),
            pltpu.VMEM((NT, SPAN, HD), bf16),
            pltpu.VMEM((NT, SPAN, HD), bf16),
            pltpu.VMEM((12, 4, SPAN, HD), f32),
            pltpu.VMEM((12, 4, SPAN, HD), f32),
            pltpu.VMEM((NT, 3 * TOK, HD), f32),
            pltpu.VMEM((NT, 3 * TOK, HD), f32),
            pltpu.VMEM((2, NT, HALF, HD), bf16),
            pltpu.VMEM((NT, TOK, HD), bf16),
            pltpu.VMEM((NT, TOK, HD), bf16),
            pltpu.VMEM((2, NT, TOK, HD), bf16),
            pltpu.VMEM((2, NT, TOK, HD), bf16),
            pltpu.VMEM((2, NT, TOK, HD), bf16),
            pltpu.VMEM((2, NT, TOK, HD), bf16),
            dma((2, NT)), dma((2, NT)),
            dma((2, NT)), dma((2, NT)),
            dma((2, 2, NT)), dma((2, 2, NT)),
            dma((8,)),
            dma((2, 2)), dma((2, 2)),
            dma((2, 2)), dma((2, 2)),
            dma((2, NT)), dma((2, NT)),
            dma((2, NT)), dma((2, NT)),
        ],
        compiler_params=pltpu.CompilerParams(
            collective_id=0, has_side_effects=True, vmem_limit_bytes=58 * 2**20
        ),
    )(head_order, time_start, height_start, log_sum_exp, row_delta, *flat)
    return tuple(x.reshape(queries.shape) for x in outs)


def solution(mesh):
    rows = P("ta", "ha", None, None)
    stats = P(None, "ta", "ha")
    return jax.shard_map(
        per_device,
        mesh=mesh,
        in_specs=(rows, rows, rows, rows, stats, stats, P(), P(), P()),
        out_specs=(rows, rows, rows),
        check_vma=False,
    )
```

```python
import functools

import jax
import jax.numpy as jnp
from jax import lax
from jax.experimental import pallas as pl
from jax.experimental.pallas import tpu as pltpu
from jax.sharding import PartitionSpec as P

HD = 128
SCALE = HD ** -0.5
LOG2E = 1.4426950408889634
NT = 16
NH = 32
TOK = 128
HALF = 64
SPAN = 3 * HALF
MESH = pl.DeviceIdType.MESH


def dot(a, b, dims):
    return lax.dot_general(a, b, (dims, ((), ())), preferred_element_type=jnp.float32)


def grads_kernel(
    order, time_start, height_start, lse, delta, queries, keys, values, out_grad,
    query_out, key_out, value_out,
    key_buf, value_buf, query_buf, grad_buf, lse_buf, delta_buf,
    key_window, value_window, probs_buf, key_parts, value_parts,
    query_low, key_low, value_low,
    key_send, value_send, key_recv, value_recv,
    stat_ss, stat_rs, kv_ss, kv_rs, qg_ss, qg_rs, own_sem,
    halo_ss, halo_rs, back_ss, back_rs, qo_ss, qo_rs, kvo_ss, kvo_rs,
):
    ta = lax.axis_index("ta")
    ha = lax.axis_index("ha")
    core = lax.rem(ha, 2)
    x_hi = lax.rem(ha // 2, 2)
    head = lax.rem(ta + 8 * x_hi, NT)

    def peer(d):
        return lax.rem(ta + d, NT)

    def head_of(p):
        return lax.rem(p + 8 * x_hi, NT)

    def columns(h):
        return pl.ds(pl.multiple_of(h * HD, HD), HD)

    left = (lax.rem(ta + 8 * (1 - core), NT), lax.rem(ha + NH - 1, NH))
    right = (lax.rem(ta + 8 * core, NT), lax.rem(ha + 1, NH))
    sides = (left, right)

    barrier = pltpu.get_barrier_semaphore()

    @pl.loop(1, NT)
    def _(d):
        pl.semaphore_signal(barrier, inc=1, device_id=(peer(d), ha), device_id_type=MESH)

    for side in sides:
        pl.semaphore_signal(barrier, inc=1, device_id=side, device_id_type=MESH)
    pl.semaphore_wait(barrier, NT + 1)

    def remote(src, dst, send_sem, recv_sem, device):
        return pltpu.make_async_remote_copy(
            src_ref=src, dst_ref=dst, send_sem=send_sem, recv_sem=recv_sem,
            device_id=device, device_id_type=MESH,
        )

    def stat_copy(n, d):
        p = peer(d)
        src, dst = ((lse, lse_buf), (delta, delta_buf))[n]
        return remote(src.at[head_of(p)], dst.at[ta], stat_ss.at[n, d], stat_rs.at[n, d], (p, ha))

    def kv_copy(n, d):
        p = peer(d)
        src, dst = ((keys, key_buf), (values, value_buf))[n]
        return remote(
            src.at[:, columns(head_of(p))], dst.at[ta, pl.ds(TOK, TOK), :],
            kv_ss.at[n, d], kv_rs.at[n, d], (p, ha),
        )

    def qg_copy(n, c, d):
        p = peer(d)
        src, dst = ((queries, query_buf), (out_grad, grad_buf))[n]
        return remote(
            src.at[pl.ds(c * HALF, HALF), columns(head_of(p))], dst.at[c, ta],
            qg_ss.at[n, c, d], qg_rs.at[n, c, d], (p, ha),
        )

    own = [
        pltpu.make_async_copy(keys.at[:, columns(head)], key_buf.at[ta, pl.ds(TOK, TOK), :], own_sem.at[0]),
        pltpu.make_async_copy(values.at[:, columns(head)], value_buf.at[ta, pl.ds(TOK, TOK), :], own_sem.at[1]),
        pltpu.make_async_copy(lse.at[head], lse_buf.at[ta], own_sem.at[2]),
        pltpu.make_async_copy(delta.at[head], delta_buf.at[ta], own_sem.at[3]),
    ]
    for c in range(2):
        for n, (src, dst) in enumerate(((queries, query_buf), (out_grad, grad_buf))):
            own.append(
                pltpu.make_async_copy(
                    src.at[pl.ds(c * HALF, HALF), columns(head)], dst.at[c, ta], own_sem.at[4 + 2 * c + n]
                )
            )

    for n in range(2):
        @pl.loop(1, NT)
        def _(d, n=n):
            kv_copy(n, d).start()
    for n in range(2):
        @pl.loop(1, NT)
        def _(d, n=n):
            stat_copy(n, d).start()
    for n in range(2):
        for c in range(2):
            @pl.loop(1, NT)
            def _(d, n=n, c=c):
                qg_copy(n, c, d).start()
    for copy in own:
        copy.start()

    for copy in own:
        copy.wait()

    halos = []
    for n, buf in enumerate((key_buf, value_buf)):
        @pl.loop(1, NT)
        def _(d, n=n):
            kv_copy(n, d).wait_recv()

        for s in range(2):
            copy = remote(
                buf.at[:, pl.ds(TOK, TOK), :],
                buf.at[:, pl.ds(2 * TOK * (1 - s), TOK), :],
                halo_ss.at[n, s], halo_rs.at[n, s], sides[s],
            )
            copy.start()
            halos.append(copy)

    model_head = order[head]

    def pick(at_head):
        entry = at_head(0)
        for m in range(1, NT):
            entry = jnp.where(model_head == m, at_head(m), entry)
        return entry

    def is_early(a):
        return pick(lambda m: time_start[a, m]) == 0

    early = [None] + [is_early(a) for a in (1, 2)]
    low_lane = lax.broadcasted_iota(jnp.int32, (1, HD), 1) < HALF

    def stat_row(buf, a, c):
        rows = [buf[4 * a + i] for i in range(4)]
        flipped = [pltpu.roll(row, HALF, 1) for row in rows]
        if c == 0:
            pairs = [jnp.where(low_lane, rows[2 * i], flipped[2 * i + 1]) for i in range(2)]
        else:
            pairs = [jnp.where(low_lane, flipped[2 * i], rows[2 * i + 1]) for i in range(2)]
        return jnp.concatenate(pairs, axis=1)

    def query_copy(c, frame):
        return remote(
            query_low.at[c, frame], query_out.at[pl.ds(c * HALF, HALF), columns(head)],
            qo_ss.at[c, frame], qo_rs.at[c, ta], (frame, ha),
        )

    def query_own(c):
        return pltpu.make_async_copy(
            query_low.at[c, ta], query_out.at[pl.ds(c * HALF, HALF), columns(head)], qo_ss.at[c, ta]
        )

    steps = [pick(lambda m, c=c: height_start[m, 2 * ha + c]) - (2 * ha + c) + 2 for c in range(2)]
    at = [[step == d for d in range(3)] for step in steps]

    def choose_height(buf, window):
        @pl.loop(0, NT)
        def _(frame):
            for c in range(2):
                spans = [buf[frame, pl.ds(HALF * (c + d), SPAN), :] for d in range(3)]
                window[c, frame] = jnp.where(at[c][0], spans[0], jnp.where(at[c][1], spans[1], spans[2]))

    def tile(window, c, soon, j):
        now = window[c, pl.ds(4 * j, 4)]
        later = window[c, pl.ds(4 * j + 4, 4)]
        return jnp.where(soon, now, later).reshape(4 * SPAN, HD)

    def tokens(buf, c, a):
        return buf[c, pl.ds(4 * a, 4)].reshape(4 * HALF, HD)

    for n in range(2):
        @pl.loop(1, NT)
        def _(d, n=n):
            stat_copy(n, d).wait_recv()

    for s in range(2):
        halos[s].wait_recv()
    choose_height(key_buf, key_window)
    for c in range(2):
        @pl.loop(1, NT)
        def _(d, c=c):
            qg_copy(0, c, d).wait_recv()

        @pl.loop(0, 4)
        def _(a, c=c):
            soon = is_early(a)
            query = tokens(query_buf, c, a)
            lse_row = stat_row(lse_buf, a, c) * LOG2E
            for j in range(3):
                scores = dot(tile(key_window, c, soon, j), query, ((1,), (1,)))
                probs_buf[4 * c + a, j] = jnp.exp2(scores * (SCALE * LOG2E) - lse_row)

    for s in range(2):
        halos[2 + s].wait_recv()
    choose_height(value_buf, value_window)

    def over_time(parts, c):
        @pl.loop(0, 4)
        def _(i):
            def entry(a, j):
                return parts[c, 3 * a + j, i]

            last = jnp.where(early[1], 0.0, entry(1, 2)) + jnp.where(early[2], 0.0, entry(2, 2))
            parts[c, 11, i] = last + entry(3, 2)
            for t in (2, 1):
                found = entry(0, t) + entry(3, t - 1)
                for a in (1, 2):
                    found = found + jnp.where(early[a], entry(a, t), entry(a, t - 1))
                parts[c, 8 + t, i] = found
            first = jnp.where(early[1], entry(1, 0), 0.0) + jnp.where(early[2], entry(2, 0), 0.0)
            parts[c, 0, i] = first + entry(0, 0)

    def piece(parts, frame, c, e):
        t = frame // 4
        place = jnp.where(t == 0, 0, 8 + t)
        found = None
        for d in range(3):
            k = e - c - d
            if 0 <= k < 3:
                got = parts[c, place, lax.rem(frame, 4), HALF * k : HALF * (k + 1), :]
                found = jnp.where(at[c][d], got, 0.0 if found is None else found)
        return found

    def around(parts, frame, e):
        found = [piece(parts, frame, c, e) for c in range(2) if 0 <= e - c < 5]
        return found[0] if len(found) == 1 else found[0] + found[1]

    back = {}

    def send_back(n, e):
        parts, send, recv = ((key_parts, key_send, key_recv), (value_parts, value_send, value_recv))[n]
        s, c = e // 4, e % 2

        @pl.loop(0, NT)
        def _(frame):
            send[s, c, frame] = around(parts, frame, e).astype(jnp.bfloat16)

        copy = remote(
            send.at[s, c], recv.at[1 - s, c], back_ss.at[n, c, s], back_rs.at[n, c, 1 - s], sides[s]
        )
        copy.start()
        back[n, c, s] = copy

    for c in range(2):
        @pl.loop(1, NT)
        def _(d, c=c):
            qg_copy(1, c, d).wait_recv()

        @pl.loop(0, 4)
        def _(a, c=c):
            soon = is_early(a)
            query = tokens(query_buf, c, a)
            grad = tokens(grad_buf, c, a)
            delta_row = stat_row(delta_buf, a, c)
            turned = jnp.zeros((HD, 4 * HALF), jnp.float32)
            for j in range(3):
                key = tile(key_window, c, soon, j)
                value = tile(value_window, c, soon, j)
                probs = probs_buf[4 * c + a, j]
                dprob = dot(value, grad, ((1,), (1,)))
                dscore = (probs * (dprob - delta_row)).astype(jnp.bfloat16)
                value_parts[c, 3 * a + j] = dot(
                    probs.astype(jnp.bfloat16), grad, ((1,), (0,))
                ).reshape(4, SPAN, HD)
                key_parts[c, 3 * a + j] = dot(dscore, query, ((1,), (0,))).reshape(4, SPAN, HD)
                turned = turned + dot(key, dscore, ((0,), (0,)))
            query_low[c, pl.ds(4 * a, 4)] = (
                (turned.T * SCALE).astype(jnp.bfloat16).reshape(4, HALF, HD)
            )
            for i in range(4):
                frame = 4 * a + i

                @pl.when(frame != ta)
                def _(frame=frame):
                    query_copy(c, frame).start()

                @pl.when(frame == ta)
                def _():
                    query_own(c).start()

        over_time(value_parts, c)
        if c == 0:
            over_time(key_parts, c)
            send_back(1, 0)
            send_back(0, 0)

    send_back(1, 4)
    send_back(1, 1)
    send_back(1, 5)
    over_time(key_parts, 1)
    send_back(0, 4)
    send_back(0, 1)
    send_back(0, 5)

    def grad_copy(n, c, d):
        p = peer(d)
        low, out = ((key_low, key_out), (value_low, value_out))[n]
        return remote(
            low.at[c, p], out.at[pl.ds(c * HALF, HALF), columns(head)],
            kvo_ss.at[n, c, d], kvo_rs.at[n, c, d], (p, ha),
        )

    own_out = []
    for n in (1, 0):
        parts, recv, low, out = (
            (key_parts, key_recv, key_low, key_out), (value_parts, value_recv, value_low, value_out)
        )[n]
        factor = SCALE if n == 0 else 1.0
        for c in range(2):
            for s in range(2):
                back[n, c, s].wait_recv()

            @pl.loop(0, NT)
            def _(frame, parts=parts, recv=recv, low=low, factor=factor, c=c):
                whole = (
                    around(parts, frame, 2 + c)
                    + recv[0, c, frame].astype(jnp.float32)
                    + recv[1, c, frame].astype(jnp.float32)
                )
                low[c, frame] = (whole * factor).astype(jnp.bfloat16)

            @pl.loop(1, NT)
            def _(d, n=n, c=c):
                grad_copy(n, c, d).start()

            copy = pltpu.make_async_copy(
                low.at[c, ta], out.at[pl.ds(c * HALF, HALF), columns(head)], own_sem.at[2 * n + c]
            )
            copy.start()
            own_out.append(copy)

    for n in range(2):
        @pl.loop(1, NT)
        def _(d, n=n):
            stat_copy(n, d).wait_send()
            kv_copy(n, d).wait_send()
            for c in range(2):
                qg_copy(n, c, d).wait_send()
    for copy in halos + list(back.values()):
        copy.wait_send()
    for c in range(2):
        query_own(c).wait()

        @pl.loop(1, NT)
        def _(d, c=c):
            frame = peer(d)
            done = remote(
                query_low.at[c, frame], query_out.at[pl.ds(c * HALF, HALF), columns(head_of(frame))],
                qo_ss.at[c, frame], qo_rs.at[c, frame], (frame, ha),
            )
            done.wait_send()
            done.wait_recv()

    for n in range(2):
        for c in range(2):
            @pl.loop(1, NT)
            def _(d, n=n, c=c):
                grad_copy(n, c, d).wait()

    for copy in own_out:
        copy.wait()


def move_kernel(*refs):
    sources, targets, buf, in_sem, out_sem = refs[:3], refs[3:6], refs[6], refs[7], refs[8]
    rows = [pl.ds(c * HALF, HALF) for c in range(2)]
    arrive = [
        pltpu.make_async_copy(sources[i].at[rows[c]], buf.at[i, rows[c]], in_sem.at[i, c])
        for i in range(3) for c in range(2)
    ]
    leave = [
        pltpu.make_async_copy(buf.at[i, rows[c]], targets[i].at[rows[c]], out_sem.at[i, c])
        for i in range(3) for c in range(2)
    ]
    for copy in arrive:
        copy.start()
    for first, second in zip(arrive, leave):
        first.wait()
        second.start()
    for copy in leave:
        copy.wait()


def per_device(
    queries, keys, values, out_grad, log_sum_exp, row_delta, time_start, height_start, head_order
):
    width = NT * HD
    flat = [x.reshape(TOK, width) for x in (queries, keys, values, out_grad)]
    smem = pl.BlockSpec(memory_space=pltpu.SMEM)
    hbm = pl.BlockSpec(memory_space=pl.ANY)
    bf16, f32 = jnp.bfloat16, jnp.float32
    dma = pltpu.SemaphoreType.DMA
    outs = pl.pallas_call(
        grads_kernel,
        name="tile_attention_grads",
        out_shape=[jax.ShapeDtypeStruct((TOK, width), bf16)] * 3,
        in_specs=[smem] * 3 + [hbm] * 6,
        out_specs=[hbm] * 3,
        scratch_shapes=[
            pltpu.VMEM((NT, 3 * TOK, HD), bf16),
            pltpu.VMEM((NT, 3 * TOK, HD), bf16),
            pltpu.VMEM((2, NT, HALF, HD), bf16),
            pltpu.VMEM((2, NT, HALF, HD), bf16),
            pltpu.VMEM((NT, 1, TOK), f32),
            pltpu.VMEM((NT, 1, TOK), f32),
            pltpu.VMEM((2, NT, SPAN, HD), bf16),
            pltpu.VMEM((2, NT, SPAN, HD), bf16),
            pltpu.VMEM((8, 3, 4 * SPAN, 4 * HALF), f32),
            pltpu.VMEM((2, 12, 4, SPAN, HD), f32),
            pltpu.VMEM((2, 12, 4, SPAN, HD), f32),
            pltpu.VMEM((2, NT, HALF, HD), bf16),
            pltpu.VMEM((2, NT, HALF, HD), bf16),
            pltpu.VMEM((2, NT, HALF, HD), bf16),
            pltpu.VMEM((2, 2, NT, HALF, HD), bf16),
            pltpu.VMEM((2, 2, NT, HALF, HD), bf16),
            pltpu.VMEM((2, 2, NT, HALF, HD), bf16),
            pltpu.VMEM((2, 2, NT, HALF, HD), bf16),
            dma((2, NT)), dma((2, NT)),
            dma((2, NT)), dma((2, NT)),
            dma((2, 2, NT)), dma((2, 2, NT)),
            dma((8,)),
            dma((2, 2)), dma((2, 2)),
            dma((2, 2, 2)), dma((2, 2, 2)),
            dma((2, NT)), dma((2, NT)),
            dma((2, 2, NT)), dma((2, 2, NT)),
        ],
        compiler_params=pltpu.CompilerParams(
            collective_id=0, has_side_effects=True, vmem_limit_bytes=60 * 2**20
        ),
    )(head_order, time_start.T, height_start, log_sum_exp, row_delta, *flat)
    outs = pl.pallas_call(
        move_kernel,
        name="place_grads",
        out_shape=[jax.ShapeDtypeStruct((TOK, width), bf16)] * 3,
        in_specs=[hbm] * 3,
        out_specs=[hbm] * 3,
        scratch_shapes=[pltpu.VMEM((3, TOK, width), bf16), dma((3, 2)), dma((3, 2))],
        compiler_params=pltpu.CompilerParams(vmem_limit_bytes=60 * 2**20),
    )(*outs)
    return tuple(x.reshape(queries.shape) for x in outs)


def solution(mesh):
    rows = P("ta", "ha", None, None)
    stats = P(None, "ta", "ha")
    return jax.shard_map(
        per_device,
        mesh=mesh,
        in_specs=(rows, rows, rows, rows, stats, stats, P(), P(), P()),
        out_specs=(rows, rows, rows),
        check_vma=False,
    )
```

```python
import functools

import jax
import jax.numpy as jnp
from jax import lax
from jax.experimental import pallas as pl
from jax.experimental.pallas import tpu as pltpu
from jax.sharding import PartitionSpec as P

HD = 128
SCALE = HD ** -0.5
LOG2E = 1.4426950408889634
NT = 16
NH = 32
TOK = 128
HALF = 64
SPAN = 3 * HALF
MESH = pl.DeviceIdType.MESH


def dot(a, b, dims):
    return lax.dot_general(a, b, (dims, ((), ())), preferred_element_type=jnp.float32)


def grads_kernel(
    order, time_start, height_start, lse, delta, queries, keys, values, out_grad,
    query_out, key_out, value_out,
    key_buf, value_buf, query_buf, grad_buf, lse_buf, delta_buf,
    key_window, value_window, probs_buf, key_parts, value_parts,
    query_low, key_low, value_low,
    key_send, value_send, key_recv, value_recv,
    stat_ss, stat_rs, kv_ss, kv_rs, qg_ss, qg_rs, own_sem,
    halo_ss, halo_rs, back_ss, back_rs, qo_ss, qo_rs, kvo_ss, kvo_rs,
):
    ta = lax.axis_index("ta")
    ha = lax.axis_index("ha")
    core = lax.rem(ha, 2)
    x_hi = lax.rem(ha // 2, 2)
    head = lax.rem(ta + 8 * x_hi, NT)

    def peer(d):
        return lax.rem(ta + d, NT)

    def head_of(p):
        return lax.rem(p + 8 * x_hi, NT)

    def columns(h):
        return pl.ds(pl.multiple_of(h * HD, HD), HD)

    left = (lax.rem(ta + 8 * (1 - core), NT), lax.rem(ha + NH - 1, NH))
    right = (lax.rem(ta + 8 * core, NT), lax.rem(ha + 1, NH))
    sides = (left, right)
    across = (lax.rem(ta + 8, NT), lax.rem(ha + NH - 1 + 2 * core, NH))
    within = (ta, ha + 1 - 2 * core)
    spot = (core, 1 - core)

    def rows_of(k):
        return pl.ds(pl.multiple_of(spot[k] * HALF, HALF), HALF)

    barrier = pltpu.get_barrier_semaphore()

    @pl.loop(1, NT)
    def _(d):
        pl.semaphore_signal(barrier, inc=1, device_id=(peer(d), ha), device_id_type=MESH)

    for side in sides:
        pl.semaphore_signal(barrier, inc=1, device_id=side, device_id_type=MESH)
    pl.semaphore_wait(barrier, NT + 1)

    def remote(src, dst, send_sem, recv_sem, device):
        return pltpu.make_async_remote_copy(
            src_ref=src, dst_ref=dst, send_sem=send_sem, recv_sem=recv_sem,
            device_id=device, device_id_type=MESH,
        )

    def stat_copy(n, d):
        p = peer(d)
        src, dst = ((lse, lse_buf), (delta, delta_buf))[n]
        return remote(src.at[head_of(p)], dst.at[ta], stat_ss.at[n, d], stat_rs.at[n, d], (p, ha))

    def kv_copy(n, d):
        p = peer(d)
        src, dst = ((keys, key_buf), (values, value_buf))[n]
        return remote(
            src.at[:, columns(head_of(p))], dst.at[ta, pl.ds(TOK, TOK), :],
            kv_ss.at[n, d], kv_rs.at[n, d], (p, ha),
        )

    def qg_copy(n, k, d):
        p = peer(d)
        src, dst = ((queries, query_buf), (out_grad, grad_buf))[n]
        return remote(
            src.at[rows_of(k), columns(head_of(p))], dst.at[k, ta],
            qg_ss.at[n, k, d], qg_rs.at[n, k, d], (p, ha),
        )

    own = [
        pltpu.make_async_copy(keys.at[:, columns(head)], key_buf.at[ta, pl.ds(TOK, TOK), :], own_sem.at[0]),
        pltpu.make_async_copy(values.at[:, columns(head)], value_buf.at[ta, pl.ds(TOK, TOK), :], own_sem.at[1]),
        pltpu.make_async_copy(lse.at[head], lse_buf.at[ta], own_sem.at[2]),
        pltpu.make_async_copy(delta.at[head], delta_buf.at[ta], own_sem.at[3]),
    ]
    for k in range(2):
        for n, (src, dst) in enumerate(((queries, query_buf), (out_grad, grad_buf))):
            own.append(
                pltpu.make_async_copy(src.at[rows_of(k), columns(head)], dst.at[k, ta], own_sem.at[4 + 2 * k + n])
            )

    for n in range(2):
        @pl.loop(1, NT)
        def _(d, n=n):
            kv_copy(n, d).start()
    for n in range(2):
        @pl.loop(1, NT)
        def _(d, n=n):
            stat_copy(n, d).start()
    for k in range(2):
        for n in range(2):
            @pl.loop(1, NT)
            def _(d, n=n, k=k):
                qg_copy(n, k, d).start()
    for copy in own:
        copy.start()

    for copy in own:
        copy.wait()

    halos = []
    for n, buf in enumerate((key_buf, value_buf)):
        @pl.loop(1, NT)
        def _(d, n=n):
            kv_copy(n, d).wait_recv()

        for s in range(2):
            copy = remote(
                buf.at[:, pl.ds(TOK, TOK), :],
                buf.at[:, pl.ds(2 * TOK * (1 - s), TOK), :],
                halo_ss.at[n, s], halo_rs.at[n, s], sides[s],
            )
            copy.start()
            halos.append(copy)

    model_head = order[head]

    def pick(at_head):
        entry = at_head(0)
        for m in range(1, NT):
            entry = jnp.where(model_head == m, at_head(m), entry)
        return entry

    def is_early(a):
        return pick(lambda m: time_start[a, m]) == 0

    early = [None] + [is_early(a) for a in (1, 2)]
    low_lane = lax.broadcasted_iota(jnp.int32, (1, HD), 1) < HALF

    def stat_row(buf, a, k):
        rows = [buf[4 * a + i] for i in range(4)]
        flipped = [pltpu.roll(row, HALF, 1) for row in rows]
        low = spot[k] == 0
        pairs = [
            jnp.where(
                low_lane,
                jnp.where(low, rows[2 * i], flipped[2 * i]),
                jnp.where(low, flipped[2 * i + 1], rows[2 * i + 1]),
            )
            for i in range(2)
        ]
        return jnp.concatenate(pairs, axis=1)

    def query_copy(k, frame):
        return remote(
            query_low.at[k, frame], query_out.at[rows_of(k), columns(head)],
            qo_ss.at[k, frame], qo_rs.at[k, ta], (frame, ha),
        )

    def query_own(k):
        return pltpu.make_async_copy(
            query_low.at[k, ta], query_out.at[rows_of(k), columns(head)], qo_ss.at[k, ta]
        )

    steps = [pick(lambda m, k=k: height_start[m, 2 * ha + spot[k]]) - (2 * ha + spot[k]) + 2 for k in range(2)]
    starts = [[step == d for d in range(3)] for step in steps]
    at = [[jnp.where(core == 0, step, 2 - step) == d for d in range(3)] for step in steps]

    def choose_height(buf, window):
        @pl.loop(0, NT)
        def _(frame):
            for k in range(2):
                spans = [
                    buf[frame, pl.ds(pl.multiple_of(HALF * (spot[k] + d), HALF), SPAN), :] for d in range(3)
                ]
                window[k, frame] = jnp.where(
                    starts[k][0], spans[0], jnp.where(starts[k][1], spans[1], spans[2])
                )

    def tile(window, k, soon, j):
        now = window[k, pl.ds(4 * j, 4)]
        later = window[k, pl.ds(4 * j + 4, 4)]
        return jnp.where(soon, now, later).reshape(4 * SPAN, HD)

    def tokens(buf, k, a):
        return buf[k, pl.ds(4 * a, 4)].reshape(4 * HALF, HD)

    def probabilities(k):
        @pl.loop(1, NT)
        def _(d):
            qg_copy(0, k, d).wait_recv()

        @pl.loop(0, 4)
        def _(a):
            soon = is_early(a)
            query = tokens(query_buf, k, a)
            lse_row = stat_row(lse_buf, a, k) * LOG2E
            for j in range(3):
                scores = dot(tile(key_window, k, soon, j), query, ((1,), (1,)))
                probs_buf[a, j] = jnp.exp2(scores * (SCALE * LOG2E) - lse_row)

    def gradients(k):
        @pl.loop(1, NT)
        def _(d):
            qg_copy(1, k, d).wait_recv()

        @pl.loop(0, 4)
        def _(a):
            soon = is_early(a)
            query = tokens(query_buf, k, a)
            grad = tokens(grad_buf, k, a)
            delta_row = stat_row(delta_buf, a, k)
            turned = jnp.zeros((HD, 4 * HALF), jnp.float32)
            for j in range(3):
                key = tile(key_window, k, soon, j)
                value = tile(value_window, k, soon, j)
                probs = probs_buf[a, j]
                dprob = dot(value, grad, ((1,), (1,)))
                dscore = (probs * (dprob - delta_row)).astype(jnp.bfloat16)
                value_parts[k, 3 * a + j] = dot(
                    probs.astype(jnp.bfloat16), grad, ((1,), (0,))
                ).reshape(4, SPAN, HD)
                key_parts[k, 3 * a + j] = dot(dscore, query, ((1,), (0,))).reshape(4, SPAN, HD)
                turned = turned + dot(key, dscore, ((0,), (0,)))
            query_low[k, pl.ds(4 * a, 4)] = (
                (turned.T * SCALE).astype(jnp.bfloat16).reshape(4, HALF, HD)
            )
            for i in range(4):
                frame = 4 * a + i

                @pl.when(frame != ta)
                def _(frame=frame):
                    query_copy(k, frame).start()

                @pl.when(frame == ta)
                def _():
                    query_own(k).start()

    def over_time(parts, k):
        @pl.loop(0, 4)
        def _(i):
            def entry(a, j):
                return parts[k, 3 * a + j, i]

            last = jnp.where(early[1], 0.0, entry(1, 2)) + jnp.where(early[2], 0.0, entry(2, 2))
            parts[k, 11, i] = last + entry(3, 2)
            for t in (2, 1):
                found = entry(0, t) + entry(3, t - 1)
                for a in (1, 2):
                    found = found + jnp.where(early[a], entry(a, t), entry(a, t - 1))
                parts[k, 8 + t, i] = found
            first = jnp.where(early[1], entry(1, 0), 0.0) + jnp.where(early[2], entry(2, 0), 0.0)
            parts[k, 0, i] = first + entry(0, 0)

    def piece(parts, frame, k, e):
        t = frame // 4
        place = jnp.where(t == 0, 0, 8 + t)
        found = None
        for d in range(3):
            w = e - k - d
            if 0 <= w < 3:
                spot_w = pl.multiple_of(HALF * (w + core * (2 - 2 * w)), HALF)
                got = parts[k, place, lax.rem(frame, 4), pl.ds(spot_w, HALF), :]
                found = jnp.where(at[k][d], got, 0.0 if found is None else found)
        return found

    def around(parts, frame, e):
        found = [piece(parts, frame, k, e) for k in range(2) if 0 <= e - k < 5]
        return found[0] if len(found) == 1 else found[0] + found[1]

    back = {}

    def send_back(n, e):
        parts, send, recv = ((key_parts, key_send, key_recv), (value_parts, value_send, value_recv))[n]
        s, k = e // 4, (e + 1) % 2

        @pl.loop(0, NT)
        def _(frame):
            send[s, k, frame] = around(parts, frame, e).astype(jnp.bfloat16)

        copy = remote(
            send.at[s, k], recv.at[s, k], back_ss.at[n, k, s], back_rs.at[n, k, s], (across, within)[s]
        )
        copy.start()
        back[n, k, s] = copy

    for n in range(2):
        @pl.loop(1, NT)
        def _(d, n=n):
            stat_copy(n, d).wait_recv()

    for s in range(2):
        halos[s].wait_recv()
    choose_height(key_buf, key_window)
    probabilities(0)
    for s in range(2):
        halos[2 + s].wait_recv()
    choose_height(value_buf, value_window)
    gradients(0)
    for n in (1, 0):
        over_time((key_parts, value_parts)[n], 0)
        send_back(n, 0)
    probabilities(1)
    gradients(1)
    for n in (1, 0):
        over_time((key_parts, value_parts)[n], 1)
        send_back(n, 4)
    for e in (1, 5):
        for n in (1, 0):
            send_back(n, e)

    def grad_copy(n, k, d):
        p = peer(d)
        low, out = ((key_low, key_out), (value_low, value_out))[n]
        return remote(
            low.at[k, p], out.at[rows_of(k), columns(head)],
            kvo_ss.at[n, k, d], kvo_rs.at[n, k, d], (p, ha),
        )

    own_out = []
    for k in (1, 0):
        for n in (1, 0):
            parts, recv, low, out = (
                (key_parts, key_recv, key_low, key_out), (value_parts, value_recv, value_low, value_out)
            )[n]
            factor = SCALE if n == 0 else 1.0
            for s in range(2):
                back[n, k, s].wait_recv()

            @pl.loop(0, NT)
            def _(frame, parts=parts, recv=recv, low=low, factor=factor, k=k):
                whole = (
                    around(parts, frame, 2 + k)
                    + recv[0, k, frame].astype(jnp.float32)
                    + recv[1, k, frame].astype(jnp.float32)
                )
                low[k, frame] = (whole * factor).astype(jnp.bfloat16)

            @pl.loop(1, NT)
            def _(d, n=n, k=k):
                grad_copy(n, k, d).start()

            copy = pltpu.make_async_copy(
                low.at[k, ta], out.at[rows_of(k), columns(head)], own_sem.at[2 * n + k]
            )
            copy.start()
            own_out.append(copy)

    for n in range(2):
        @pl.loop(1, NT)
        def _(d, n=n):
            stat_copy(n, d).wait_send()
            kv_copy(n, d).wait_send()
            for k in range(2):
                qg_copy(n, k, d).wait_send()
    for copy in halos + list(back.values()):
        copy.wait_send()
    for k in range(2):
        query_own(k).wait()

        @pl.loop(1, NT)
        def _(d, k=k):
            frame = peer(d)
            done = remote(
                query_low.at[k, frame], query_out.at[rows_of(k), columns(head_of(frame))],
                qo_ss.at[k, frame], qo_rs.at[k, frame], (frame, ha),
            )
            done.wait_send()
            done.wait_recv()

    for n in range(2):
        for k in range(2):
            @pl.loop(1, NT)
            def _(d, n=n, k=k):
                grad_copy(n, k, d).wait()

    for copy in own_out:
        copy.wait()


def move_kernel(*refs):
    sources, targets, buf, in_sem, out_sem = refs[:3], refs[3:6], refs[6], refs[7], refs[8]
    rows = [pl.ds(c * HALF, HALF) for c in range(2)]
    arrive = [
        pltpu.make_async_copy(sources[i].at[rows[c]], buf.at[i, rows[c]], in_sem.at[i, c])
        for i in range(3) for c in range(2)
    ]
    leave = [
        pltpu.make_async_copy(buf.at[i, rows[c]], targets[i].at[rows[c]], out_sem.at[i, c])
        for i in range(3) for c in range(2)
    ]
    for copy in arrive:
        copy.start()
    for first, second in zip(arrive, leave):
        first.wait()
        second.start()
    for copy in leave:
        copy.wait()


def per_device(
    queries, keys, values, out_grad, log_sum_exp, row_delta, time_start, height_start, head_order
):
    width = NT * HD
    flat = [x.reshape(TOK, width) for x in (queries, keys, values, out_grad)]
    smem = pl.BlockSpec(memory_space=pltpu.SMEM)
    hbm = pl.BlockSpec(memory_space=pl.ANY)
    bf16, f32 = jnp.bfloat16, jnp.float32
    dma = pltpu.SemaphoreType.DMA
    outs = pl.pallas_call(
        grads_kernel,
        name="tile_attention_grads",
        out_shape=[jax.ShapeDtypeStruct((TOK, width), bf16)] * 3,
        in_specs=[smem] * 3 + [hbm] * 6,
        out_specs=[hbm] * 3,
        scratch_shapes=[
            pltpu.VMEM((NT, 3 * TOK, HD), bf16),
            pltpu.VMEM((NT, 3 * TOK, HD), bf16),
            pltpu.VMEM((2, NT, HALF, HD), bf16),
            pltpu.VMEM((2, NT, HALF, HD), bf16),
            pltpu.VMEM((NT, 1, TOK), f32),
            pltpu.VMEM((NT, 1, TOK), f32),
            pltpu.VMEM((2, NT, SPAN, HD), bf16),
            pltpu.VMEM((2, NT, SPAN, HD), bf16),
            pltpu.VMEM((4, 3, 4 * SPAN, 4 * HALF), f32),
            pltpu.VMEM((2, 12, 4, SPAN, HD), f32),
            pltpu.VMEM((2, 12, 4, SPAN, HD), f32),
            pltpu.VMEM((2, NT, HALF, HD), bf16),
            pltpu.VMEM((2, NT, HALF, HD), bf16),
            pltpu.VMEM((2, NT, HALF, HD), bf16),
            pltpu.VMEM((2, 2, NT, HALF, HD), bf16),
            pltpu.VMEM((2, 2, NT, HALF, HD), bf16),
            pltpu.VMEM((2, 2, NT, HALF, HD), bf16),
            pltpu.VMEM((2, 2, NT, HALF, HD), bf16),
            dma((2, NT)), dma((2, NT)),
            dma((2, NT)), dma((2, NT)),
            dma((2, 2, NT)), dma((2, 2, NT)),
            dma((8,)),
            dma((2, 2)), dma((2, 2)),
            dma((2, 2, 2)), dma((2, 2, 2)),
            dma((2, NT)), dma((2, NT)),
            dma((2, 2, NT)), dma((2, 2, NT)),
        ],
        compiler_params=pltpu.CompilerParams(
            collective_id=0, has_side_effects=True, vmem_limit_bytes=60 * 2**20
        ),
    )(head_order, time_start.T, height_start, log_sum_exp, row_delta, *flat)
    outs = pl.pallas_call(
        move_kernel,
        name="place_grads",
        out_shape=[jax.ShapeDtypeStruct((TOK, width), bf16)] * 3,
        in_specs=[hbm] * 3,
        out_specs=[hbm] * 3,
        scratch_shapes=[pltpu.VMEM((3, TOK, width), bf16), dma((3, 2)), dma((3, 2))],
        compiler_params=pltpu.CompilerParams(vmem_limit_bytes=60 * 2**20),
    )(*outs)
    return tuple(x.reshape(queries.shape) for x in outs)


def solution(mesh):
    rows = P("ta", "ha", None, None)
    stats = P(None, "ta", "ha")
    return jax.shard_map(
        per_device,
        mesh=mesh,
        in_specs=(rows, rows, rows, rows, stats, stats, P(), P(), P()),
        out_specs=(rows, rows, rows),
        check_vma=False,
    )
```

```python
import functools

import jax
import jax.numpy as jnp
from jax import lax
from jax.experimental import pallas as pl
from jax.experimental.pallas import tpu as pltpu
from jax.sharding import PartitionSpec as P

HD = 128
SCALE = HD ** -0.5
LOG2E = 1.4426950408889634
NT = 16
NH = 32
TOK = 128
HALF = 64
SPAN = 3 * HALF
MESH = pl.DeviceIdType.MESH


def dot(a, b, dims):
    return lax.dot_general(a, b, (dims, ((), ())), preferred_element_type=jnp.float32)


def grads_kernel(
    order, time_start, height_start, lse, delta, queries, keys, values, out_grad,
    query_out, pair_out,
    qg_stage, stat_stage, key_buf, value_buf, qg_buf, stat_buf,
    key_window, value_window, probs_buf, key_parts, value_parts,
    query_low, pair_low, inner_low,
    key_send, value_send, key_recv, value_recv,
    stat_ss, stat_rs, kv_ss, kv_rs, qg_ss, qg_rs, own_sem,
    halo_ss, halo_rs, back_ss, back_rs, qo_ss, qo_rs, kvo_ss, kvo_rs,
):
    ta = lax.axis_index("ta")
    ha = lax.axis_index("ha")
    core = lax.rem(ha, 2)
    x_hi = lax.rem(ha // 2, 2)
    head = lax.rem(ta + 8 * x_hi, NT)

    def peer(d):
        return lax.rem(ta + d, NT)

    def head_of(p):
        return lax.rem(p + 8 * x_hi, NT)

    def columns(h):
        return pl.ds(pl.multiple_of(h * HD, HD), HD)

    left = (lax.rem(ta + 8 * (1 - core), NT), lax.rem(ha + NH - 1, NH))
    right = (lax.rem(ta + 8 * core, NT), lax.rem(ha + 1, NH))
    sides = (left, right)
    across = (lax.rem(ta + 8, NT), lax.rem(ha + NH - 1 + 2 * core, NH))
    within = (ta, ha + 1 - 2 * core)
    spot = (core, 1 - core)

    def rows_of(k):
        return pl.ds(pl.multiple_of(spot[k] * HALF, HALF), HALF)

    barrier = pltpu.get_barrier_semaphore()

    @pl.loop(1, NT)
    def _(d):
        pl.semaphore_signal(barrier, inc=1, device_id=(peer(d), ha), device_id_type=MESH)

    for side in sides:
        pl.semaphore_signal(barrier, inc=1, device_id=side, device_id_type=MESH)
    pl.semaphore_wait(barrier, NT + 1)

    def remote(src, dst, send_sem, recv_sem, device):
        return pltpu.make_async_remote_copy(
            src_ref=src, dst_ref=dst, send_sem=send_sem, recv_sem=recv_sem,
            device_id=device, device_id_type=MESH,
        )

    def stat_copy(d):
        p = peer(d)
        return remote(stat_stage.at[head_of(p)], stat_buf.at[ta], stat_ss.at[d], stat_rs.at[d], (p, ha))

    def kv_copy(n, d):
        p = peer(d)
        src, dst = ((keys, key_buf), (values, value_buf))[n]
        return remote(
            src.at[:, columns(head_of(p))], dst.at[ta, pl.ds(TOK, TOK), :],
            kv_ss.at[n, d], kv_rs.at[n, d], (p, ha),
        )

    def qg_copy(k, d):
        p = peer(d)
        return remote(
            qg_stage.at[k, :, :, columns(head_of(p))], qg_buf.at[k, ta],
            qg_ss.at[k, d], qg_rs.at[k, d], (p, ha),
        )

    staged = [
        pltpu.make_async_copy(src, stat_stage.at[:, n], own_sem.at[n]) for n, src in enumerate((lse, delta))
    ]
    for k in range(2):
        for n, src in enumerate((queries, out_grad)):
            staged.append(pltpu.make_async_copy(src.at[rows_of(k), :], qg_stage.at[k, n], own_sem.at[2 + 2 * k + n]))
    for copy in staged:
        copy.start()

    for n in range(2):
        @pl.loop(1, NT)
        def _(d, n=n):
            kv_copy(n, d).start()

    own = [
        pltpu.make_async_copy(keys.at[:, columns(head)], key_buf.at[ta, pl.ds(TOK, TOK), :], own_sem.at[6]),
        pltpu.make_async_copy(values.at[:, columns(head)], value_buf.at[ta, pl.ds(TOK, TOK), :], own_sem.at[7]),
    ]
    for copy in own:
        copy.start()
    for copy in staged:
        copy.wait()

    @pl.loop(1, NT)
    def _(d):
        stat_copy(d).start()

    for k in range(2):
        @pl.loop(1, NT)
        def _(d, k=k):
            qg_copy(k, d).start()

    own.append(pltpu.make_async_copy(stat_stage.at[head], stat_buf.at[ta], own_sem.at[0]))
    for k in range(2):
        own.append(
            pltpu.make_async_copy(qg_stage.at[k, :, :, columns(head)], qg_buf.at[k, ta], own_sem.at[1 + k])
        )
    for copy in own[2:]:
        copy.start()
    for copy in own:
        copy.wait()

    halos = []
    for n, buf in enumerate((key_buf, value_buf)):
        @pl.loop(1, NT)
        def _(d, n=n):
            kv_copy(n, d).wait_recv()

        for s in range(2):
            copy = remote(
                buf.at[:, pl.ds(TOK, TOK), :],
                buf.at[:, pl.ds(2 * TOK * (1 - s), TOK), :],
                halo_ss.at[n, s], halo_rs.at[n, s], sides[s],
            )
            copy.start()
            halos.append(copy)

    model_head = order[head]

    def pick(at_head):
        entry = at_head(0)
        for m in range(1, NT):
            entry = jnp.where(model_head == m, at_head(m), entry)
        return entry

    def is_early(a):
        return pick(lambda m: time_start[a, m]) == 0

    early = [is_early(a) for a in range(4)]

    def soon_of(a):
        return jnp.where(a < 2, jnp.where(a == 0, early[0], early[1]), jnp.where(a == 2, early[2], early[3]))

    low_lane = lax.broadcasted_iota(jnp.int32, (1, HD), 1) < HALF

    def stat_row(n, a, k):
        rows = [stat_buf[4 * a + i, n] for i in range(4)]
        flipped = [pltpu.roll(row, HALF, 1) for row in rows]
        low = spot[k] == 0
        pairs = [
            jnp.where(
                low_lane,
                jnp.where(low, rows[2 * i], flipped[2 * i]),
                jnp.where(low, flipped[2 * i + 1], rows[2 * i + 1]),
            )
            for i in range(2)
        ]
        return jnp.concatenate(pairs, axis=1)

    def query_copy(k, frame):
        return remote(
            query_low.at[k, frame], query_out.at[rows_of(k), columns(head)],
            qo_ss.at[k, frame], qo_rs.at[k, ta], (frame, ha),
        )

    def query_own(k):
        return pltpu.make_async_copy(
            query_low.at[k, ta], query_out.at[rows_of(k), columns(head)], qo_ss.at[k, ta]
        )

    steps = [pick(lambda m, k=k: height_start[m, 2 * ha + spot[k]]) - (2 * ha + spot[k]) + 2 for k in range(2)]
    starts = [[step == d for d in range(3)] for step in steps]
    at = [[jnp.where(core == 0, step, 2 - step) == d for d in range(3)] for step in steps]

    def choose_height(buf, window):
        @pl.loop(0, NT)
        def _(frame):
            for k in range(2):
                spans = [
                    buf[frame, pl.ds(pl.multiple_of(HALF * (spot[k] + d), HALF), SPAN), :] for d in range(3)
                ]
                window[k, frame] = jnp.where(
                    starts[k][0], spans[0], jnp.where(starts[k][1], spans[1], spans[2])
                )

    def tile(window, k, soon, j):
        now = window[k, pl.ds(4 * j, 4)]
        later = window[k, pl.ds(4 * j + 4, 4)]
        return jnp.where(soon, now, later).reshape(4 * SPAN, HD)

    def tokens(n, k, a):
        return qg_buf[k, pl.ds(4 * a, 4), n].reshape(4 * HALF, HD)

    def send_queries(k):
        @pl.loop(1, NT)
        def _(d):
            query_copy(k, peer(d)).start()

        query_own(k).start()

    def probabilities(k):
        @pl.loop(1, NT)
        def _(d):
            qg_copy(k, d).wait_recv()

        if k == 1:
            send_queries(0)

        @pl.loop(0, 4)
        def _(a):
            soon = soon_of(a)
            query = tokens(0, k, a)
            lse_row = stat_row(0, a, k) * LOG2E
            grad = tokens(1, k, a)
            for j in range(3):
                scores = dot(tile(key_window, k, soon, j), query, ((1,), (1,)))
                probs = jnp.exp2(scores * (SCALE * LOG2E) - lse_row)
                probs_buf[a, j] = probs
                value_parts[k, 3 * a + j] = dot(
                    probs.astype(jnp.bfloat16), grad, ((1,), (0,))
                ).reshape(4, SPAN, HD)

    def gradients(k, first, last):
        @pl.loop(first, last)
        def _(step):
            a = lax.rem(step + ta // 4, 4)
            soon = soon_of(a)
            query = tokens(0, k, a)
            grad = tokens(1, k, a)
            delta_row = stat_row(1, a, k)
            turned = jnp.zeros((HD, 4 * HALF), jnp.float32)
            for j in range(3):
                key = tile(key_window, k, soon, j)
                value = tile(value_window, k, soon, j)
                probs = probs_buf[a, j]
                dprob = dot(value, grad, ((1,), (1,)))
                dscore = (probs * (dprob - delta_row)).astype(jnp.bfloat16)
                key_parts[k, 3 * a + j] = dot(dscore, query, ((1,), (0,))).reshape(4, SPAN, HD)
                turned = turned + dot(key, dscore, ((0,), (0,)))
            query_low[k, pl.ds(4 * a, 4)] = (
                (turned.T * SCALE).astype(jnp.bfloat16).reshape(4, HALF, HD)
            )
            if k == 1:
                for i in range(4):
                    frame = 4 * a + lax.rem(ta + i, 4)

                    @pl.when(frame != ta)
                    def _(frame=frame):
                        query_copy(k, frame).start()

                    @pl.when(frame == ta)
                    def _():
                        query_own(k).start()

    def over_time(parts, k):
        @pl.loop(0, 4)
        def _(i):
            def entry(a, j):
                return parts[k, 3 * a + j, i]

            last = jnp.where(early[1], 0.0, entry(1, 2)) + jnp.where(early[2], 0.0, entry(2, 2))
            parts[k, 11, i] = last + entry(3, 2)
            for t in (2, 1):
                found = entry(0, t) + entry(3, t - 1)
                for a in (1, 2):
                    found = found + jnp.where(early[a], entry(a, t), entry(a, t - 1))
                parts[k, 8 + t, i] = found
            first = jnp.where(early[1], entry(1, 0), 0.0) + jnp.where(early[2], entry(2, 0), 0.0)
            parts[k, 0, i] = first + entry(0, 0)

    def piece(parts, frame, k, e):
        t = frame // 4
        place = jnp.where(t == 0, 0, 8 + t)
        found = None
        for d in range(3):
            w = e - k - d
            if 0 <= w < 3:
                spot_w = pl.multiple_of(HALF * (w + core * (2 - 2 * w)), HALF)
                got = parts[k, place, lax.rem(frame, 4), pl.ds(spot_w, HALF), :]
                found = jnp.where(at[k][d], got, 0.0 if found is None else found)
        return found

    def around(parts, frame, e):
        found = [piece(parts, frame, k, e) for k in range(2) if 0 <= e - k < 5]
        return found[0] if len(found) == 1 else found[0] + found[1]

    back = {}

    def send_back(n, e):
        parts, send, recv = ((key_parts, key_send, key_recv), (value_parts, value_send, value_recv))[n]
        s, k = e // 4, (e + 1) % 2

        @pl.loop(0, NT)
        def _(frame):
            send[s, k, frame] = around(parts, frame, e).astype(jnp.bfloat16)

        copy = remote(
            send.at[s, k], recv.at[s, k], back_ss.at[n, k, s], back_rs.at[n, k, s], (across, within)[s]
        )
        copy.start()
        back[n, k, s] = copy

    def grad_ends(part):
        low, out = ((pair_low.at[0], pair_out.at[:, rows_of(0), columns(head)]),
                    (inner_low.at[1], pair_out.at[1, rows_of(1), columns(head)]),
                    (inner_low.at[0], pair_out.at[0, rows_of(1), columns(head)]))[part]
        return low, out

    def grad_copy(part, d):
        p = peer(d)
        low, out = grad_ends(part)
        return remote(low.at[p], out, kvo_ss.at[part, d], kvo_rs.at[part, d], (p, ha))

    own_out = []

    def add_up(n, k, low):
        parts, recv, factor = ((key_parts, key_recv, SCALE), (value_parts, value_recv, 1.0))[n]
        for s in range(2):
            back[n, k, s].wait_recv()

        @pl.loop(0, NT)
        def _(frame):
            whole = (
                around(parts, frame, 2 + k)
                + recv[0, k, frame].astype(jnp.float32)
                + recv[1, k, frame].astype(jnp.float32)
            )
            low(frame)[...] = (whole * factor).astype(jnp.bfloat16)

    def leave(part):
        @pl.loop(1, NT)
        def _(d):
            grad_copy(part, d).start()

        low, out = grad_ends(part)
        copy = pltpu.make_async_copy(low.at[ta], out, own_sem.at[part])
        copy.start()
        own_out.append(copy)

    def finish_inner(n):
        add_up(n, 1, lambda frame: inner_low.at[n, frame])
        leave(2 - n)

    def finish_outer():
        for n in (1, 0):
            add_up(n, 0, lambda frame, n=n: pair_low.at[0, frame, n])
        leave(0)

    @pl.loop(1, NT)
    def _(d):
        stat_copy(d).wait_recv()

    for s in range(2):
        halos[s].wait_recv()
    choose_height(key_buf, key_window)
    probabilities(0)
    over_time(value_parts, 0)
    send_back(1, 0)
    for s in range(2):
        halos[2 + s].wait_recv()
    choose_height(value_buf, value_window)
    gradients(0, 0, 4)
    over_time(key_parts, 0)
    send_back(0, 0)
    probabilities(1)
    over_time(value_parts, 1)
    send_back(1, 1)
    send_back(1, 4)
    gradients(1, 0, 2)
    finish_inner(1)
    gradients(1, 2, 4)
    over_time(key_parts, 1)
    send_back(0, 1)
    send_back(0, 4)
    send_back(1, 5)
    send_back(0, 5)
    finish_inner(0)
    finish_outer()

    for n in range(2):
        @pl.loop(1, NT)
        def _(d, n=n):
            qg_copy(n, d).wait_send()
            kv_copy(n, d).wait_send()

    @pl.loop(1, NT)
    def _(d):
        stat_copy(d).wait_send()

    for copy in halos + list(back.values()):
        copy.wait_send()
    for k in range(2):
        query_own(k).wait()

        @pl.loop(1, NT)
        def _(d, k=k):
            frame = peer(d)
            done = remote(
                query_low.at[k, frame], query_out.at[rows_of(k), columns(head_of(frame))],
                qo_ss.at[k, frame], qo_rs.at[k, frame], (frame, ha),
            )
            done.wait_send()
            done.wait_recv()

    for part in (1, 2, 0):
        @pl.loop(1, NT)
        def _(d, part=part):
            grad_copy(part, d).wait()

    for copy in own_out:
        copy.wait()


def move_kernel(query, pair, *refs):
    targets, buf, in_sem, out_sem = refs[:3], refs[3], refs[4], refs[5]
    sources = (query, pair.at[0], pair.at[1])
    rows = [pl.ds(c * HALF, HALF) for c in range(2)]
    arrive = [
        pltpu.make_async_copy(sources[i].at[rows[c]], buf.at[i, rows[c]], in_sem.at[i, c])
        for i in range(3) for c in range(2)
    ]
    leave = [
        pltpu.make_async_copy(buf.at[i, rows[c]], targets[i].at[rows[c]], out_sem.at[i, c])
        for i in range(3) for c in range(2)
    ]
    for copy in arrive:
        copy.start()
    for first, second in zip(arrive, leave):
        first.wait()
        second.start()
    for copy in leave:
        copy.wait()


def per_device(
    queries, keys, values, out_grad, log_sum_exp, row_delta, time_start, height_start, head_order
):
    width = NT * HD
    flat = [x.reshape(TOK, width) for x in (queries, keys, values, out_grad)]
    smem = pl.BlockSpec(memory_space=pltpu.SMEM)
    hbm = pl.BlockSpec(memory_space=pl.ANY)
    bf16, f32 = jnp.bfloat16, jnp.float32
    dma = pltpu.SemaphoreType.DMA
    outs = pl.pallas_call(
        grads_kernel,
        name="tile_attention_grads",
        out_shape=[jax.ShapeDtypeStruct((TOK, width), bf16), jax.ShapeDtypeStruct((2, TOK, width), bf16)],
        in_specs=[smem] * 3 + [hbm] * 6,
        out_specs=[hbm] * 2,
        scratch_shapes=[
            pltpu.VMEM((2, 2, HALF, width), bf16),
            pltpu.VMEM((NT, 2, 1, TOK), f32),
            pltpu.VMEM((NT, 3 * TOK, HD), bf16),
            pltpu.VMEM((NT, 3 * TOK, HD), bf16),
            pltpu.VMEM((2, NT, 2, HALF, HD), bf16),
            pltpu.VMEM((NT, 2, 1, TOK), f32),
            pltpu.VMEM((2, NT, SPAN, HD), bf16),
            pltpu.VMEM((2, NT, SPAN, HD), bf16),
            pltpu.VMEM((4, 3, 4 * SPAN, 4 * HALF), f32),
            pltpu.VMEM((2, 12, 4, SPAN, HD), f32),
            pltpu.VMEM((2, 12, 4, SPAN, HD), f32),
            pltpu.VMEM((2, NT, HALF, HD), bf16),
            pltpu.VMEM((1, NT, 2, HALF, HD), bf16),
            pltpu.VMEM((2, NT, HALF, HD), bf16),
            pltpu.VMEM((2, 2, NT, HALF, HD), bf16),
            pltpu.VMEM((2, 2, NT, HALF, HD), bf16),
            pltpu.VMEM((2, 2, NT, HALF, HD), bf16),
            pltpu.VMEM((2, 2, NT, HALF, HD), bf16),
            dma((NT,)), dma((NT,)),
            dma((2, NT)), dma((2, NT)),
            dma((2, NT)), dma((2, NT)),
            dma((8,)),
            dma((2, 2)), dma((2, 2)),
            dma((2, 2, 2)), dma((2, 2, 2)),
            dma((2, NT)), dma((2, NT)),
            dma((3, NT)), dma((3, NT)),
        ],
        compiler_params=pltpu.CompilerParams(
            collective_id=0, has_side_effects=True, vmem_limit_bytes=60 * 2**20
        ),
    )(head_order, time_start.T, height_start, log_sum_exp, row_delta, *flat)
    outs = pl.pallas_call(
        move_kernel,
        name="place_grads",
        out_shape=[jax.ShapeDtypeStruct((TOK, width), bf16)] * 3,
        in_specs=[hbm] * 2,
        out_specs=[hbm] * 3,
        scratch_shapes=[pltpu.VMEM((3, TOK, width), bf16), dma((3, 2)), dma((3, 2))],
        compiler_params=pltpu.CompilerParams(vmem_limit_bytes=60 * 2**20),
    )(*outs)
    return tuple(x.reshape(queries.shape) for x in outs)


def solution(mesh):
    rows = P("ta", "ha", None, None)
    stats = P(None, "ta", "ha")
    return jax.shard_map(
        per_device,
        mesh=mesh,
        in_specs=(rows, rows, rows, rows, stats, stats, P(), P(), P()),
        out_specs=(rows, rows, rows),
        check_vma=False,
    )
```

```python
import functools

import jax
import jax.numpy as jnp
from jax import lax
from jax.experimental import pallas as pl
from jax.experimental.pallas import tpu as pltpu
from jax.sharding import PartitionSpec as P

HD = 128
SCALE = HD ** -0.5
LOG2E = 1.4426950408889634
NT = 16
NH = 32
TOK = 128
HALF = 64
SPAN = 3 * HALF
MESH = pl.DeviceIdType.MESH


def dot(a, b, dims):
    return lax.dot_general(a, b, (dims, ((), ())), preferred_element_type=jnp.float32)


def grads_kernel(
    order, time_start, height_start, lse, delta, queries, keys, values, out_grad,
    query_out, pair_out,
    qg_stage, stat_stage, key_buf, value_buf, qg_buf, stat_buf,
    key_window, value_window, probs_buf, key_parts, value_parts,
    query_low, pair_low, inner_low,
    key_send, value_send, key_recv, value_recv,
    stat_ss, stat_rs, kv_ss, kv_rs, qg_ss, qg_rs, own_sem,
    halo_ss, halo_rs, back_ss, back_rs, qo_ss, qo_rs, kvo_ss, kvo_rs,
):
    ta = lax.axis_index("ta")
    ha = lax.axis_index("ha")
    core = lax.rem(ha, 2)
    x_hi = lax.rem(ha // 2, 2)
    head = lax.rem(ta + 8 * x_hi, NT)

    def peer(d):
        return lax.rem(ta + d, NT)

    def head_of(p):
        return lax.rem(p + 8 * x_hi, NT)

    def columns(h):
        return pl.ds(pl.multiple_of(h * HD, HD), HD)

    left = (lax.rem(ta + 8 * (1 - core), NT), lax.rem(ha + NH - 1, NH))
    right = (lax.rem(ta + 8 * core, NT), lax.rem(ha + 1, NH))
    sides = (left, right)
    across = (lax.rem(ta + 8, NT), lax.rem(ha + NH - 1 + 2 * core, NH))
    within = (ta, ha + 1 - 2 * core)
    spot = (core, 1 - core)

    def rows_of(k):
        return pl.ds(pl.multiple_of(spot[k] * HALF, HALF), HALF)

    barrier = pltpu.get_barrier_semaphore()

    @pl.loop(1, NT)
    def _(d):
        pl.semaphore_signal(barrier, inc=1, device_id=(peer(d), ha), device_id_type=MESH)

    for side in sides:
        pl.semaphore_signal(barrier, inc=1, device_id=side, device_id_type=MESH)
    staged = [
        pltpu.make_async_copy(src, stat_stage.at[:, n], own_sem.at[n]) for n, src in enumerate((lse, delta))
    ]
    for k in range(2):
        for n, src in enumerate((queries, out_grad)):
            staged.append(pltpu.make_async_copy(src.at[rows_of(k), :], qg_stage.at[k, n], own_sem.at[2 + 2 * k + n]))
    for copy in staged:
        copy.start()

    pl.semaphore_wait(barrier, NT + 1)

    def remote(src, dst, send_sem, recv_sem, device):
        return pltpu.make_async_remote_copy(
            src_ref=src, dst_ref=dst, send_sem=send_sem, recv_sem=recv_sem,
            device_id=device, device_id_type=MESH,
        )

    def stat_copy(d):
        p = peer(d)
        return remote(stat_stage.at[head_of(p)], stat_buf.at[ta], stat_ss.at[d], stat_rs.at[d], (p, ha))

    def kv_copy(n, d):
        p = peer(d)
        src, dst = ((keys, key_buf), (values, value_buf))[n]
        return remote(
            src.at[:, columns(head_of(p))], dst.at[ta, pl.ds(TOK, TOK), :],
            kv_ss.at[n, d], kv_rs.at[n, d], (p, ha),
        )

    def qg_copy(k, d):
        p = peer(d)
        return remote(
            qg_stage.at[k, :, :, columns(head_of(p))], qg_buf.at[k, ta],
            qg_ss.at[k, d], qg_rs.at[k, d], (p, ha),
        )

    for n in range(2):
        @pl.loop(1, NT)
        def _(d, n=n):
            kv_copy(n, d).start()

    own = [
        pltpu.make_async_copy(keys.at[:, columns(head)], key_buf.at[ta, pl.ds(TOK, TOK), :], own_sem.at[6]),
        pltpu.make_async_copy(values.at[:, columns(head)], value_buf.at[ta, pl.ds(TOK, TOK), :], own_sem.at[7]),
    ]
    for copy in own:
        copy.start()
    for copy in staged:
        copy.wait()

    @pl.loop(1, NT)
    def _(d):
        stat_copy(d).start()

    for k in range(2):
        @pl.loop(1, NT)
        def _(d, k=k):
            qg_copy(k, d).start()

    own.append(pltpu.make_async_copy(stat_stage.at[head], stat_buf.at[ta], own_sem.at[0]))
    for k in range(2):
        own.append(
            pltpu.make_async_copy(qg_stage.at[k, :, :, columns(head)], qg_buf.at[k, ta], own_sem.at[1 + k])
        )
    for copy in own[2:]:
        copy.start()
    for copy in own:
        copy.wait()

    halos = []
    for n, buf in enumerate((key_buf, value_buf)):
        @pl.loop(1, NT)
        def _(d, n=n):
            kv_copy(n, d).wait_recv()

        for s in range(2):
            copy = remote(
                buf.at[:, pl.ds(TOK, TOK), :],
                buf.at[:, pl.ds(2 * TOK * (1 - s), TOK), :],
                halo_ss.at[n, s], halo_rs.at[n, s], sides[s],
            )
            copy.start()
            halos.append(copy)

    model_head = order[head]

    def pick(at_head):
        entry = at_head(0)
        for m in range(1, NT):
            entry = jnp.where(model_head == m, at_head(m), entry)
        return entry

    def is_early(a):
        return pick(lambda m: time_start[a, m]) == 0

    early = [is_early(a) for a in range(4)]

    def soon_of(a):
        return jnp.where(a < 2, jnp.where(a == 0, early[0], early[1]), jnp.where(a == 2, early[2], early[3]))

    low_lane = lax.broadcasted_iota(jnp.int32, (1, HD), 1) < HALF

    def stat_row(n, a, k):
        rows = [stat_buf[4 * a + i, n] for i in range(4)]
        flipped = [pltpu.roll(row, HALF, 1) for row in rows]
        low = spot[k] == 0
        pairs = [
            jnp.where(
                low_lane,
                jnp.where(low, rows[2 * i], flipped[2 * i]),
                jnp.where(low, flipped[2 * i + 1], rows[2 * i + 1]),
            )
            for i in range(2)
        ]
        return jnp.concatenate(pairs, axis=1)

    def query_copy(k, frame):
        return remote(
            query_low.at[k, frame], query_out.at[rows_of(k), columns(head)],
            qo_ss.at[k, frame], qo_rs.at[k, ta], (frame, ha),
        )

    def query_own(k):
        return pltpu.make_async_copy(
            query_low.at[k, ta], query_out.at[rows_of(k), columns(head)], qo_ss.at[k, ta]
        )

    steps = [pick(lambda m, k=k: height_start[m, 2 * ha + spot[k]]) - (2 * ha + spot[k]) + 2 for k in range(2)]
    starts = [[step == d for d in range(3)] for step in steps]
    at = [[jnp.where(core == 0, step, 2 - step) == d for d in range(3)] for step in steps]

    def choose_height(buf, window):
        @pl.loop(0, NT)
        def _(frame):
            for k in range(2):
                spans = [
                    buf[frame, pl.ds(pl.multiple_of(HALF * (spot[k] + d), HALF), SPAN), :] for d in range(3)
                ]
                window[k, frame] = jnp.where(
                    starts[k][0], spans[0], jnp.where(starts[k][1], spans[1], spans[2])
                )

    def tile(window, k, soon, j):
        now = window[k, pl.ds(4 * j, 4)]
        later = window[k, pl.ds(4 * j + 4, 4)]
        return jnp.where(soon, now, later).reshape(4 * SPAN, HD)

    def tokens(n, k, a):
        return qg_buf[k, pl.ds(4 * a, 4), n].reshape(4 * HALF, HD)

    def send_queries(k):
        @pl.loop(1, NT)
        def _(d):
            query_copy(k, peer(d)).start()

        query_own(k).start()

    def probabilities(k):
        @pl.loop(1, NT)
        def _(d):
            qg_copy(k, d).wait_recv()

        if k == 1:
            send_queries(0)

        @pl.loop(0, 4, unroll=2)
        def _(a):
            soon = soon_of(a)
            query = tokens(0, k, a)
            lse_row = stat_row(0, a, k) * LOG2E
            grad = tokens(1, k, a)
            for j in range(3):
                scores = dot(tile(key_window, k, soon, j), query, ((1,), (1,)))
                probs = jnp.exp2(scores * (SCALE * LOG2E) - lse_row)
                probs_buf[a, j] = probs
                value_parts[k, 3 * a + j] = dot(
                    probs.astype(jnp.bfloat16), grad, ((1,), (0,))
                ).reshape(4, SPAN, HD)

    def gradients(k, first, last):
        @pl.loop(first, last, unroll=2)
        def _(step):
            a = lax.rem(step + ta // 4, 4)
            soon = soon_of(a)
            query = tokens(0, k, a)
            grad = tokens(1, k, a)
            delta_row = stat_row(1, a, k)
            turned = jnp.zeros((HD, 4 * HALF), jnp.float32)
            for j in range(3):
                key = tile(key_window, k, soon, j)
                value = tile(value_window, k, soon, j)
                probs = probs_buf[a, j]
                dprob = dot(value, grad, ((1,), (1,)))
                dscore = (probs * (dprob - delta_row)).astype(jnp.bfloat16)
                key_parts[k, 3 * a + j] = dot(dscore, query, ((1,), (0,))).reshape(4, SPAN, HD)
                turned = turned + dot(key, dscore, ((0,), (0,)))
            query_low[k, pl.ds(4 * a, 4)] = (
                (turned.T * SCALE).astype(jnp.bfloat16).reshape(4, HALF, HD)
            )
            if k == 1:
                for i in range(4):
                    frame = 4 * a + lax.rem(ta + i, 4)

                    @pl.when(frame != ta)
                    def _(frame=frame):
                        query_copy(k, frame).start()

                    @pl.when(frame == ta)
                    def _():
                        query_own(k).start()

    def over_time(parts, k):
        @pl.loop(0, 4, unroll=2)
        def _(i):
            def entry(a, j):
                return parts[k, 3 * a + j, i]

            last = jnp.where(early[1], 0.0, entry(1, 2)) + jnp.where(early[2], 0.0, entry(2, 2))
            parts[k, 11, i] = last + entry(3, 2)
            for t in (2, 1):
                found = entry(0, t) + entry(3, t - 1)
                for a in (1, 2):
                    found = found + jnp.where(early[a], entry(a, t), entry(a, t - 1))
                parts[k, 8 + t, i] = found
            first = jnp.where(early[1], entry(1, 0), 0.0) + jnp.where(early[2], entry(2, 0), 0.0)
            parts[k, 0, i] = first + entry(0, 0)

    def piece(parts, frame, k, e):
        t = frame // 4
        place = jnp.where(t == 0, 0, 8 + t)
        found = None
        for d in range(3):
            w = e - k - d
            if 0 <= w < 3:
                spot_w = pl.multiple_of(HALF * (w + core * (2 - 2 * w)), HALF)
                got = parts[k, place, lax.rem(frame, 4), pl.ds(spot_w, HALF), :]
                found = jnp.where(at[k][d], got, 0.0 if found is None else found)
        return found

    def around(parts, frame, e):
        found = [piece(parts, frame, k, e) for k in range(2) if 0 <= e - k < 5]
        return found[0] if len(found) == 1 else found[0] + found[1]

    back = {}

    def send_back(n, e):
        parts, send, recv = ((key_parts, key_send, key_recv), (value_parts, value_send, value_recv))[n]
        s, k = e // 4, (e + 1) % 2

        @pl.loop(0, NT, unroll=4)
        def _(frame):
            send[s, k, frame] = around(parts, frame, e).astype(jnp.bfloat16)

        copy = remote(
            send.at[s, k], recv.at[s, k], back_ss.at[n, k, s], back_rs.at[n, k, s], (across, within)[s]
        )
        copy.start()
        back[n, k, s] = copy

    def grad_ends(part):
        low, out = ((pair_low.at[0], pair_out.at[:, rows_of(0), columns(head)]),
                    (inner_low.at[1], pair_out.at[1, rows_of(1), columns(head)]),
                    (inner_low.at[0], pair_out.at[0, rows_of(1), columns(head)]))[part]
        return low, out

    def grad_copy(part, d):
        p = peer(d)
        low, out = grad_ends(part)
        return remote(low.at[p], out, kvo_ss.at[part, d], kvo_rs.at[part, d], (p, ha))

    own_out = []

    def add_up(n, k, low):
        parts, recv, factor = ((key_parts, key_recv, SCALE), (value_parts, value_recv, 1.0))[n]
        for s in range(2):
            back[n, k, s].wait_recv()

        @pl.loop(0, NT, unroll=4)
        def _(frame):
            whole = (
                around(parts, frame, 2 + k)
                + recv[0, k, frame].astype(jnp.float32)
                + recv[1, k, frame].astype(jnp.float32)
            )
            low(frame)[...] = (whole * factor).astype(jnp.bfloat16)

    def leave(part):
        @pl.loop(1, NT)
        def _(d):
            grad_copy(part, d).start()

        low, out = grad_ends(part)
        copy = pltpu.make_async_copy(low.at[ta], out, own_sem.at[part])
        copy.start()
        own_out.append(copy)

    def finish_inner(n):
        add_up(n, 1, lambda frame: inner_low.at[n, frame])
        leave(2 - n)

    def finish_outer():
        for n in (1, 0):
            add_up(n, 0, lambda frame, n=n: pair_low.at[0, frame, n])
        leave(0)

    @pl.loop(1, NT)
    def _(d):
        stat_copy(d).wait_recv()

    for s in range(2):
        halos[s].wait_recv()
    choose_height(key_buf, key_window)
    probabilities(0)
    over_time(value_parts, 0)
    send_back(1, 0)
    for s in range(2):
        halos[2 + s].wait_recv()
    choose_height(value_buf, value_window)
    gradients(0, 0, 4)
    over_time(key_parts, 0)
    send_back(0, 0)
    probabilities(1)
    over_time(value_parts, 1)
    send_back(1, 1)
    send_back(1, 4)
    gradients(1, 0, 2)
    finish_inner(1)
    gradients(1, 2, 4)
    over_time(key_parts, 1)
    send_back(0, 1)
    send_back(0, 4)
    finish_inner(0)
    send_back(1, 5)
    send_back(0, 5)
    finish_outer()

    for n in range(2):
        @pl.loop(1, NT)
        def _(d, n=n):
            qg_copy(n, d).wait_send()
            kv_copy(n, d).wait_send()

    @pl.loop(1, NT)
    def _(d):
        stat_copy(d).wait_send()

    for copy in halos + list(back.values()):
        copy.wait_send()
    for k in range(2):
        query_own(k).wait()

        @pl.loop(1, NT)
        def _(d, k=k):
            frame = peer(d)
            done = remote(
                query_low.at[k, frame], query_out.at[rows_of(k), columns(head_of(frame))],
                qo_ss.at[k, frame], qo_rs.at[k, frame], (frame, ha),
            )
            done.wait_send()
            done.wait_recv()

    for part in (1, 2, 0):
        @pl.loop(1, NT)
        def _(d, part=part):
            grad_copy(part, d).wait()

    for copy in own_out:
        copy.wait()


def move_kernel(query, pair, *refs):
    targets, buf, in_sem, out_sem = refs[:3], refs[3], refs[4], refs[5]
    sources = (query, pair.at[0], pair.at[1])
    rows = [pl.ds(c * HALF, HALF) for c in range(2)]
    arrive = [
        pltpu.make_async_copy(sources[i].at[rows[c]], buf.at[i, rows[c]], in_sem.at[i, c])
        for i in range(3) for c in range(2)
    ]
    leave = [
        pltpu.make_async_copy(buf.at[i, rows[c]], targets[i].at[rows[c]], out_sem.at[i, c])
        for i in range(3) for c in range(2)
    ]
    for copy in arrive:
        copy.start()
    for first, second in zip(arrive, leave):
        first.wait()
        second.start()
    for copy in leave:
        copy.wait()


def per_device(
    queries, keys, values, out_grad, log_sum_exp, row_delta, time_start, height_start, head_order
):
    width = NT * HD
    flat = [x.reshape(TOK, width) for x in (queries, keys, values, out_grad)]
    smem = pl.BlockSpec(memory_space=pltpu.SMEM)
    hbm = pl.BlockSpec(memory_space=pl.ANY)
    bf16, f32 = jnp.bfloat16, jnp.float32
    dma = pltpu.SemaphoreType.DMA
    outs = pl.pallas_call(
        grads_kernel,
        name="tile_attention_grads",
        out_shape=[jax.ShapeDtypeStruct((TOK, width), bf16), jax.ShapeDtypeStruct((2, TOK, width), bf16)],
        in_specs=[smem] * 3 + [hbm] * 6,
        out_specs=[hbm] * 2,
        scratch_shapes=[
            pltpu.VMEM((2, 2, HALF, width), bf16),
            pltpu.VMEM((NT, 2, 1, TOK), f32),
            pltpu.VMEM((NT, 3 * TOK, HD), bf16),
            pltpu.VMEM((NT, 3 * TOK, HD), bf16),
            pltpu.VMEM((2, NT, 2, HALF, HD), bf16),
            pltpu.VMEM((NT, 2, 1, TOK), f32),
            pltpu.VMEM((2, NT, SPAN, HD), bf16),
            pltpu.VMEM((2, NT, SPAN, HD), bf16),
            pltpu.VMEM((4, 3, 4 * SPAN, 4 * HALF), f32),
            pltpu.VMEM((2, 12, 4, SPAN, HD), f32),
            pltpu.VMEM((2, 12, 4, SPAN, HD), f32),
            pltpu.VMEM((2, NT, HALF, HD), bf16),
            pltpu.VMEM((1, NT, 2, HALF, HD), bf16),
            pltpu.VMEM((2, NT, HALF, HD), bf16),
            pltpu.VMEM((2, 2, NT, HALF, HD), bf16),
            pltpu.VMEM((2, 2, NT, HALF, HD), bf16),
            pltpu.VMEM((2, 2, NT, HALF, HD), bf16),
            pltpu.VMEM((2, 2, NT, HALF, HD), bf16),
            dma((NT,)), dma((NT,)),
            dma((2, NT)), dma((2, NT)),
            dma((2, NT)), dma((2, NT)),
            dma((8,)),
            dma((2, 2)), dma((2, 2)),
            dma((2, 2, 2)), dma((2, 2, 2)),
            dma((2, NT)), dma((2, NT)),
            dma((3, NT)), dma((3, NT)),
        ],
        compiler_params=pltpu.CompilerParams(
            collective_id=0, has_side_effects=True, vmem_limit_bytes=60 * 2**20
        ),
    )(head_order, time_start.T, height_start, log_sum_exp, row_delta, *flat)
    outs = pl.pallas_call(
        move_kernel,
        name="place_grads",
        out_shape=[jax.ShapeDtypeStruct((TOK, width), bf16)] * 3,
        in_specs=[hbm] * 2,
        out_specs=[hbm] * 3,
        scratch_shapes=[pltpu.VMEM((3, TOK, width), bf16), dma((3, 2)), dma((3, 2))],
        compiler_params=pltpu.CompilerParams(vmem_limit_bytes=60 * 2**20),
    )(*outs)
    return tuple(x.reshape(queries.shape) for x in outs)


def solution(mesh):
    rows = P("ta", "ha", None, None)
    stats = P(None, "ta", "ha")
    return jax.shard_map(
        per_device,
        mesh=mesh,
        in_specs=(rows, rows, rows, rows, stats, stats, P(), P(), P()),
        out_specs=(rows, rows, rows),
        check_vma=False,
    )
```

```python
import functools

import jax
import jax.numpy as jnp
from jax import lax
from jax.experimental import pallas as pl
from jax.experimental.pallas import tpu as pltpu
from jax.sharding import PartitionSpec as P

HD = 128
SCALE = HD ** -0.5
LOG2E = 1.4426950408889634
NT = 16
NH = 32
TOK = 128
HALF = 64
SPAN = 3 * HALF
MESH = pl.DeviceIdType.MESH


def dot(a, b, dims):
    return lax.dot_general(a, b, (dims, ((), ())), preferred_element_type=jnp.float32)


def grads_kernel(
    order, time_start, height_start, lse, delta, queries, keys, values, out_grad,
    query_out, pair_out,
    qg_stage, stat_stage, key_buf, value_buf, qg_buf, stat_buf,
    key_window, value_window, probs_buf, key_parts, value_parts,
    query_low, pair_low, inner_low,
    key_send, value_send, key_recv, value_recv,
    stat_ss, stat_rs, kv_ss, kv_rs, qg_ss, qg_rs, own_sem,
    halo_ss, halo_rs, back_ss, back_rs, qo_ss, qo_rs, kvo_ss, kvo_rs,
):
    ta = lax.axis_index("ta")
    ha = lax.axis_index("ha")
    core = lax.rem(ha, 2)
    x_hi = lax.rem(ha // 2, 2)
    head = lax.rem(ta + 8 * x_hi, NT)

    def peer(d):
        return lax.rem(ta + d, NT)

    def head_of(p):
        return lax.rem(p + 8 * x_hi, NT)

    def columns(h):
        return pl.ds(pl.multiple_of(h * HD, HD), HD)

    left = (lax.rem(ta + 8 * (1 - core), NT), lax.rem(ha + NH - 1, NH))
    right = (lax.rem(ta + 8 * core, NT), lax.rem(ha + 1, NH))
    sides = (left, right)
    across = (lax.rem(ta + 8, NT), lax.rem(ha + NH - 1 + 2 * core, NH))
    within = (ta, ha + 1 - 2 * core)
    spot = (core, 1 - core)

    def rows_of(k):
        return pl.ds(pl.multiple_of(spot[k] * HALF, HALF), HALF)

    barrier = pltpu.get_barrier_semaphore()

    @pl.loop(1, NT)
    def _(d):
        pl.semaphore_signal(barrier, inc=1, device_id=(peer(d), ha), device_id_type=MESH)

    for side in sides:
        pl.semaphore_signal(barrier, inc=1, device_id=side, device_id_type=MESH)
    staged = [
        pltpu.make_async_copy(src, stat_stage.at[:, n], own_sem.at[n]) for n, src in enumerate((lse, delta))
    ]
    for k in range(2):
        for n, src in enumerate((queries, out_grad)):
            staged.append(pltpu.make_async_copy(src.at[rows_of(k), :], qg_stage.at[k, n], own_sem.at[2 + 2 * k + n]))
    for copy in staged:
        copy.start()

    pl.semaphore_wait(barrier, NT + 1)

    def remote(src, dst, send_sem, recv_sem, device):
        return pltpu.make_async_remote_copy(
            src_ref=src, dst_ref=dst, send_sem=send_sem, recv_sem=recv_sem,
            device_id=device, device_id_type=MESH,
        )

    def stat_copy(d):
        p = peer(d)
        return remote(stat_stage.at[head_of(p)], stat_buf.at[ta], stat_ss.at[d], stat_rs.at[d], (p, ha))

    def kv_copy(n, d):
        p = peer(d)
        src, dst = ((keys, key_buf), (values, value_buf))[n]
        return remote(
            src.at[:, columns(head_of(p))], dst.at[ta, pl.ds(TOK, TOK), :],
            kv_ss.at[n, d], kv_rs.at[n, d], (p, ha),
        )

    def qg_copy(k, d):
        p = peer(d)
        return remote(
            qg_stage.at[k, :, :, columns(head_of(p))], qg_buf.at[k, ta],
            qg_ss.at[k, d], qg_rs.at[k, d], (p, ha),
        )

    for n in range(2):
        @pl.loop(1, NT)
        def _(d, n=n):
            kv_copy(n, d).start()

    own = [
        pltpu.make_async_copy(keys.at[:, columns(head)], key_buf.at[ta, pl.ds(TOK, TOK), :], own_sem.at[6]),
        pltpu.make_async_copy(values.at[:, columns(head)], value_buf.at[ta, pl.ds(TOK, TOK), :], own_sem.at[7]),
    ]
    for copy in own:
        copy.start()
    for copy in staged:
        copy.wait()

    @pl.loop(1, NT)
    def _(d):
        stat_copy(d).start()

    for k in range(2):
        @pl.loop(1, NT)
        def _(d, k=k):
            qg_copy(k, d).start()

    own.append(pltpu.make_async_copy(stat_stage.at[head], stat_buf.at[ta], own_sem.at[0]))
    for k in range(2):
        own.append(
            pltpu.make_async_copy(qg_stage.at[k, :, :, columns(head)], qg_buf.at[k, ta], own_sem.at[1 + k])
        )
    for copy in own[2:]:
        copy.start()
    for copy in own:
        copy.wait()

    halos = []
    for n, buf in enumerate((key_buf, value_buf)):
        @pl.loop(1, NT)
        def _(d, n=n):
            kv_copy(n, d).wait_recv()

        for s in range(2):
            copy = remote(
                buf.at[:, pl.ds(TOK, TOK), :],
                buf.at[:, pl.ds(2 * TOK * (1 - s), TOK), :],
                halo_ss.at[n, s], halo_rs.at[n, s], sides[s],
            )
            copy.start()
            halos.append(copy)

    model_head = order[head]

    def pick(at_head):
        entry = at_head(0)
        for m in range(1, NT):
            entry = jnp.where(model_head == m, at_head(m), entry)
        return entry

    def is_early(a):
        return pick(lambda m: time_start[a, m]) == 0

    early = [is_early(a) for a in range(4)]

    def soon_of(a):
        return jnp.where(a < 2, jnp.where(a == 0, early[0], early[1]), jnp.where(a == 2, early[2], early[3]))

    low_lane = lax.broadcasted_iota(jnp.int32, (1, HD), 1) < HALF

    def stat_row(n, a, k):
        rows = [stat_buf[4 * a + i, n] for i in range(4)]
        flipped = [pltpu.roll(row, HALF, 1) for row in rows]
        low = spot[k] == 0
        pairs = [
            jnp.where(
                low_lane,
                jnp.where(low, rows[2 * i], flipped[2 * i]),
                jnp.where(low, flipped[2 * i + 1], rows[2 * i + 1]),
            )
            for i in range(2)
        ]
        return jnp.concatenate(pairs, axis=1)

    def query_copy(k, frame):
        return remote(
            query_low.at[k, frame], query_out.at[rows_of(k), columns(head)],
            qo_ss.at[k, frame], qo_rs.at[k, ta], (frame, ha),
        )

    def query_own(k):
        return pltpu.make_async_copy(
            query_low.at[k, ta], query_out.at[rows_of(k), columns(head)], qo_ss.at[k, ta]
        )

    steps = [pick(lambda m, k=k: height_start[m, 2 * ha + spot[k]]) - (2 * ha + spot[k]) + 2 for k in range(2)]
    starts = [[step == d for d in range(3)] for step in steps]
    at = [[jnp.where(core == 0, step, 2 - step) == d for d in range(3)] for step in steps]

    def choose_height(buf, window):
        @pl.loop(0, NT)
        def _(frame):
            for k in range(2):
                spans = [
                    buf[frame, pl.ds(pl.multiple_of(HALF * (spot[k] + d), HALF), SPAN), :] for d in range(3)
                ]
                window[k, frame] = jnp.where(
                    starts[k][0], spans[0], jnp.where(starts[k][1], spans[1], spans[2])
                )

    def tile(window, k, soon, j):
        now = window[k, pl.ds(4 * j, 4)]
        later = window[k, pl.ds(4 * j + 4, 4)]
        return jnp.where(soon, now, later).reshape(4 * SPAN, HD)

    def tokens(n, k, a):
        return qg_buf[k, pl.ds(4 * a, 4), n].reshape(4 * HALF, HD)

    def send_queries(k):
        @pl.loop(1, NT)
        def _(d):
            query_copy(k, peer(d)).start()

        query_own(k).start()

    def probabilities(k):
        @pl.loop(1, NT)
        def _(d):
            qg_copy(k, d).wait_recv()

        if k == 1:
            send_queries(0)

        @pl.loop(0, 4, unroll=2)
        def _(a):
            soon = soon_of(a)
            query = tokens(0, k, a)
            lse_row = stat_row(0, a, k) * LOG2E
            grad = tokens(1, k, a)
            for j in range(3):
                scores = dot(tile(key_window, k, soon, j), query, ((1,), (1,)))
                probs = jnp.exp2(scores * (SCALE * LOG2E) - lse_row)
                probs_buf[a, j] = probs
                value_parts[k, 3 * a + j] = dot(
                    probs.astype(jnp.bfloat16), grad, ((1,), (0,))
                ).reshape(4, SPAN, HD)

    def gradients(k, first, last):
        @pl.loop(first, last, unroll=2)
        def _(step):
            a = lax.rem(step + ta // 4, 4)
            soon = soon_of(a)
            query = tokens(0, k, a)
            grad = tokens(1, k, a)
            delta_row = stat_row(1, a, k)
            turned = jnp.zeros((HD, 4 * HALF), jnp.float32)
            for j in range(3):
                key = tile(key_window, k, soon, j)
                value = tile(value_window, k, soon, j)
                probs = probs_buf[a, j]
                dprob = dot(value, grad, ((1,), (1,)))
                dscore = (probs * (dprob - delta_row)).astype(jnp.bfloat16)
                key_parts[k, 3 * a + j] = dot(dscore, query, ((1,), (0,))).reshape(4, SPAN, HD)
                turned = turned + dot(key, dscore, ((0,), (0,)))
            query_low[k, pl.ds(4 * a, 4)] = (
                (turned.T * SCALE).astype(jnp.bfloat16).reshape(4, HALF, HD)
            )
            if k == 1:
                for i in range(4):
                    frame = 4 * a + lax.rem(ta + i, 4)

                    @pl.when(frame != ta)
                    def _(frame=frame):
                        query_copy(k, frame).start()

                    @pl.when(frame == ta)
                    def _():
                        query_own(k).start()

    def over_time(parts, k):
        @pl.loop(0, 4, unroll=2)
        def _(i):
            def entry(a, j):
                return parts[k, 3 * a + j, i]

            last = jnp.where(early[1], 0.0, entry(1, 2)) + jnp.where(early[2], 0.0, entry(2, 2))
            parts[k, 11, i] = last + entry(3, 2)
            for t in (2, 1):
                found = entry(0, t) + entry(3, t - 1)
                for a in (1, 2):
                    found = found + jnp.where(early[a], entry(a, t), entry(a, t - 1))
                parts[k, 8 + t, i] = found
            first = jnp.where(early[1], entry(1, 0), 0.0) + jnp.where(early[2], entry(2, 0), 0.0)
            parts[k, 0, i] = first + entry(0, 0)

    def piece(parts, frame, k, e):
        t = frame // 4
        place = jnp.where(t == 0, 0, 8 + t)
        found = None
        for d in range(3):
            w = e - k - d
            if 0 <= w < 3:
                spot_w = pl.multiple_of(HALF * (w + core * (2 - 2 * w)), HALF)
                got = parts[k, place, lax.rem(frame, 4), pl.ds(spot_w, HALF), :]
                found = jnp.where(at[k][d], got, 0.0 if found is None else found)
        return found

    def around(parts, frame, e):
        found = [piece(parts, frame, k, e) for k in range(2) if 0 <= e - k < 5]
        return found[0] if len(found) == 1 else found[0] + found[1]

    back = {}

    def send_back(n, e):
        parts, send, recv = ((key_parts, key_send, key_recv), (value_parts, value_send, value_recv))[n]
        s, k = e // 4, (e + 1) % 2

        @pl.loop(0, NT, unroll=4)
        def _(frame):
            send[s, k, frame] = around(parts, frame, e).astype(jnp.bfloat16)

        copy = remote(
            send.at[s, k], recv.at[s, k], back_ss.at[n, k, s], back_rs.at[n, k, s], (across, within)[s]
        )
        copy.start()
        back[n, k, s] = copy

    def grad_ends(part):
        low, out = ((pair_low.at[0], pair_out.at[:, rows_of(0), columns(head)]),
                    (inner_low.at[1], pair_out.at[1, rows_of(1), columns(head)]),
                    (inner_low.at[0], pair_out.at[0, rows_of(1), columns(head)]))[part]
        return low, out

    def grad_copy(part, d):
        p = peer(d)
        low, out = grad_ends(part)
        return remote(low.at[p], out, kvo_ss.at[part, d], kvo_rs.at[part, d], (p, ha))

    own_out = []

    def add_up(n, k, low):
        parts, recv, factor = ((key_parts, key_recv, SCALE), (value_parts, value_recv, 1.0))[n]
        for s in range(2):
            back[n, k, s].wait_recv()

        @pl.loop(0, NT, unroll=4)
        def _(frame):
            whole = (
                around(parts, frame, 2 + k)
                + recv[0, k, frame].astype(jnp.float32)
                + recv[1, k, frame].astype(jnp.float32)
            )
            low(frame)[...] = (whole * factor).astype(jnp.bfloat16)

    def leave(part):
        @pl.loop(1, NT)
        def _(d):
            grad_copy(part, d).start()

        low, out = grad_ends(part)
        copy = pltpu.make_async_copy(low.at[ta], out, own_sem.at[part])
        copy.start()
        own_out.append(copy)

    def finish_inner(n):
        add_up(n, 1, lambda frame: inner_low.at[n, frame])
        leave(2 - n)

    def finish_outer():
        for n in (1, 0):
            add_up(n, 0, lambda frame, n=n: pair_low.at[0, frame, n])
        leave(0)

    @pl.loop(1, NT)
    def _(d):
        stat_copy(d).wait_recv()

    for s in range(2):
        halos[s].wait_recv()
    choose_height(key_buf, key_window)
    probabilities(0)
    over_time(value_parts, 0)
    send_back(1, 0)
    for s in range(2):
        halos[2 + s].wait_recv()
    choose_height(value_buf, value_window)
    gradients(0, 0, 4)
    over_time(key_parts, 0)
    send_back(0, 0)
    probabilities(1)
    over_time(value_parts, 1)
    send_back(1, 4)
    send_back(1, 1)
    gradients(1, 0, 2)
    finish_inner(1)
    gradients(1, 2, 4)
    over_time(key_parts, 1)
    send_back(0, 4)
    send_back(0, 1)
    finish_inner(0)
    send_back(1, 5)
    send_back(0, 5)
    finish_outer()

    for n in range(2):
        @pl.loop(1, NT)
        def _(d, n=n):
            qg_copy(n, d).wait_send()
            kv_copy(n, d).wait_send()

    @pl.loop(1, NT)
    def _(d):
        stat_copy(d).wait_send()

    for copy in halos + list(back.values()):
        copy.wait_send()
    for k in range(2):
        query_own(k).wait()

        @pl.loop(1, NT)
        def _(d, k=k):
            frame = peer(d)
            done = remote(
                query_low.at[k, frame], query_out.at[rows_of(k), columns(head_of(frame))],
                qo_ss.at[k, frame], qo_rs.at[k, frame], (frame, ha),
            )
            done.wait_send()
            done.wait_recv()

    for part in (1, 2, 0):
        @pl.loop(1, NT)
        def _(d, part=part):
            grad_copy(part, d).wait()

    for copy in own_out:
        copy.wait()


def move_kernel(query, pair, *refs):
    targets, buf, in_sem, out_sem = refs[:3], refs[3], refs[4], refs[5]
    sources = (query, pair.at[0], pair.at[1])
    rows = [pl.ds(c * HALF, HALF) for c in range(2)]
    arrive = [
        pltpu.make_async_copy(sources[i].at[rows[c]], buf.at[i, rows[c]], in_sem.at[i, c])
        for i in range(3) for c in range(2)
    ]
    leave = [
        pltpu.make_async_copy(buf.at[i, rows[c]], targets[i].at[rows[c]], out_sem.at[i, c])
        for i in range(3) for c in range(2)
    ]
    for copy in arrive:
        copy.start()
    for first, second in zip(arrive, leave):
        first.wait()
        second.start()
    for copy in leave:
        copy.wait()


def per_device(
    queries, keys, values, out_grad, log_sum_exp, row_delta, time_start, height_start, head_order
):
    width = NT * HD
    flat = [x.reshape(TOK, width) for x in (queries, keys, values, out_grad)]
    smem = pl.BlockSpec(memory_space=pltpu.SMEM)
    hbm = pl.BlockSpec(memory_space=pl.ANY)
    bf16, f32 = jnp.bfloat16, jnp.float32
    dma = pltpu.SemaphoreType.DMA
    outs = pl.pallas_call(
        grads_kernel,
        name="tile_attention_grads",
        out_shape=[jax.ShapeDtypeStruct((TOK, width), bf16), jax.ShapeDtypeStruct((2, TOK, width), bf16)],
        in_specs=[smem] * 3 + [hbm] * 6,
        out_specs=[hbm] * 2,
        scratch_shapes=[
            pltpu.VMEM((2, 2, HALF, width), bf16),
            pltpu.VMEM((NT, 2, 1, TOK), f32),
            pltpu.VMEM((NT, 3 * TOK, HD), bf16),
            pltpu.VMEM((NT, 3 * TOK, HD), bf16),
            pltpu.VMEM((2, NT, 2, HALF, HD), bf16),
            pltpu.VMEM((NT, 2, 1, TOK), f32),
            pltpu.VMEM((2, NT, SPAN, HD), bf16),
            pltpu.VMEM((2, NT, SPAN, HD), bf16),
            pltpu.VMEM((4, 3, 4 * SPAN, 4 * HALF), f32),
            pltpu.VMEM((2, 12, 4, SPAN, HD), f32),
            pltpu.VMEM((2, 12, 4, SPAN, HD), f32),
            pltpu.VMEM((2, NT, HALF, HD), bf16),
            pltpu.VMEM((1, NT, 2, HALF, HD), bf16),
            pltpu.VMEM((2, NT, HALF, HD), bf16),
            pltpu.VMEM((2, 2, NT, HALF, HD), bf16),
            pltpu.VMEM((2, 2, NT, HALF, HD), bf16),
            pltpu.VMEM((2, 2, NT, HALF, HD), bf16),
            pltpu.VMEM((2, 2, NT, HALF, HD), bf16),
            dma((NT,)), dma((NT,)),
            dma((2, NT)), dma((2, NT)),
            dma((2, NT)), dma((2, NT)),
            dma((8,)),
            dma((2, 2)), dma((2, 2)),
            dma((2, 2, 2)), dma((2, 2, 2)),
            dma((2, NT)), dma((2, NT)),
            dma((3, NT)), dma((3, NT)),
        ],
        compiler_params=pltpu.CompilerParams(
            collective_id=0, has_side_effects=True, vmem_limit_bytes=60 * 2**20
        ),
    )(head_order, time_start.T, height_start, log_sum_exp, row_delta, *flat)
    outs = pl.pallas_call(
        move_kernel,
        name="place_grads",
        out_shape=[jax.ShapeDtypeStruct((TOK, width), bf16)] * 3,
        in_specs=[hbm] * 2,
        out_specs=[hbm] * 3,
        scratch_shapes=[pltpu.VMEM((3, TOK, width), bf16), dma((3, 2)), dma((3, 2))],
        compiler_params=pltpu.CompilerParams(vmem_limit_bytes=60 * 2**20),
    )(*outs)
    return tuple(x.reshape(queries.shape) for x in outs)


def solution(mesh):
    rows = P("ta", "ha", None, None)
    stats = P(None, "ta", "ha")
    return jax.shard_map(
        per_device,
        mesh=mesh,
        in_specs=(rows, rows, rows, rows, stats, stats, P(), P(), P()),
        out_specs=(rows, rows, rows),
        check_vma=False,
    )
```
